32 devices in a mesh: row: 8 (over z, x), col: 4 (over y, core).
Axes of the slice: x: 2, y: 2, z: 4, core: 2. Of those that a mesh axis runs over, the one named last changes fastest.
Arguments:
- interaction: bfloat16 [5, 8192, 8192], P(None, 'row', 'col'), may hold values from -0.0390625 to 0.0390625
- history_currents: bfloat16 [4, 8192, 512], P(None, ('col', 'row')), may hold values from -5 to 5
- incident: float32 [2, 8192, 512], P(None, ('row', 'col')), may hold values from -4 to 4
- load_gain: float32 [8192], P('row'), may hold values from 0.5 to 1.5
- load_cubic: float32 [8192], P('row'), may hold values from 0.005 to 0.04
- delays: int32 [8, 4, 5], P('row', 'col'), may hold values from 1 to 4
- tile_map: int32 [8, 4], P('row', 'col'), may hold values 0 or 1
Outputs:
- currents: bfloat16 [2, 8192, 512], P(None, ('row', 'col'))
The draws below stay inside these ranges and needn't reach their ends.
Inputs may be any that keep to these rules, and one draw needn't show every extreme that they name: Slot k of tile (r, c) reads the current of delays[r, c, k] steps before the marched step.
All inputs are finite; a program needn't handle non-finite values. No bound on the sum of `tile_map` on one device may be relied on, other than what follows from the above.
Results may differ from the reference program's by a relative error of at most 0.0024.
Values may be sent and summed in bfloat16 or wider, within the bound.
No kernel may reach another device: no remote copies, remote signals or barrier semaphores. Data moves between devices by JAX's collectives and lax.ppermute only.
A program may use at most 128 MiB of HBM per device.

```python
import math
import jax
import jax.numpy as jnp
from jax import lax

W = 512
K = 5
H = 4
STEPS = 2
N = 8192
N_ROW = 8
N_COL = 4


def with_ends(entries, key, smallest, largest):
    dims = entries.shape
    place = [jax.random.randint(jax.random.fold_in(key, axis), (), 0, dims[axis]) for axis in range(len(dims))]
    entries = entries.at[tuple(place)].set(smallest)
    longest = dims.index(max(dims))
    place[longest] = (place[longest] + 1) % dims[longest]
    return entries.at[tuple(place)].set(largest)


def strengthened(array, rng, source, target, parts, factor):
    def block_of(dim):
        return (jnp.arange(array.shape[dim]) // (array.shape[dim] // parts)).reshape((-1,) + (1,) * (array.ndim - 1 - dim))

    near = jax.random.permutation(rng, parts)[block_of(target)]
    second = (block_of(target) + parts // 2) % parts
    return jnp.where((block_of(source) == near) | (block_of(source) == second), factor * array, array)


def block_scale(rng, extent, split, low, high):
    loudness, own = 1.0, jax.random.fold_in(rng, 6)
    for dim, shards_of in split:
        steps = jnp.exp(jax.random.uniform(jax.random.fold_in(own, dim), (shards_of,), jnp.float32, low / len(split), high / len(split)))
        loudness = loudness * jnp.repeat(steps, extent[dim] // shards_of).reshape([-1 if axis == dim else 1 for axis in range(len(extent))])
    return loudness


def noise(stream_key, dims, width, limit, split=(), kind=jnp.bfloat16):
    entries = width * jax.random.normal(stream_key, dims, jnp.float32)
    if split:
        entries = entries * block_scale(stream_key, dims, split, -0.22, 0.18)
    return jnp.clip(entries, -limit, limit).astype(kind)


def noise_with(rng, extent, deviation, limit, split, heavy, held_as=jnp.bfloat16):
    entries = deviation * jax.random.normal(rng, extent, jnp.float32)
    if split:
        entries = entries * block_scale(rng, extent, split, -0.22, 0.18)
    return jnp.clip(strengthened(entries, jax.random.fold_in(rng, 3), *heavy), -limit, limit).astype(held_as)


def setup_inputs(seed: int = 0) -> dict:
    keys = jax.random.split(jax.random.key(seed), 8)
    return {
        "interaction": noise_with(keys[0], (K, N, N), (K * N) ** -0.5, 0.0390625, ((1, 8), (2, 4)), (2, 1, 8, 2.0)),
        "history_currents": noise(keys[1], (H, N, W), 1.0, 5.0, ((1, 32),)),
        "incident": noise(keys[2], (STEPS, N, W), 0.7, 4.0, ((1, 32),), jnp.float32),
        "load_gain": jnp.clip(1.0 + 0.1 * jax.random.normal(keys[3], (N,), jnp.float32), 0.5, 1.5),
        "load_cubic": jnp.clip(jnp.exp(math.log(0.04) - 2.0794415 * jax.random.uniform(keys[4], (N,), jnp.float32) ** block_scale(keys[4], (N,), ((0, 8),), -0.2, 0.2)), 0.005, 0.04),
        "delays": with_ends(jax.random.randint(keys[5], (N_ROW, N_COL, K), 1, H + 1), jax.random.fold_in(keys[5], 1), 1, H).astype(jnp.int32),
        "tile_map": with_ends((jax.random.randint(keys[6], (N_ROW, N_COL), 0, 4) < 3).astype(jnp.int32), jax.random.fold_in(keys[6], 1), 0, 1),
    }


def reference(interaction, history_currents, incident, load_gain, load_cubic, delays, tile_map):
    block_obs = N // N_ROW
    block_src = N // N_COL
    buffer = jnp.concatenate([history_currents, jnp.zeros((STEPS, N, W), jnp.bfloat16)], axis=0)
    results = []
    for instant in range(STEPS):
        shaped = buffer.reshape(H + STEPS, N_COL, block_src, W)

        def row_field(row_number):
            zrow = lax.dynamic_slice_in_dim(interaction, row_number * block_obs, block_obs, 1)
            zrow = zrow.astype(jnp.float32).reshape(K, block_obs, N_COL, block_src)
            position = (H + instant - delays[row_number]).astype(jnp.int32)
            columns = jnp.arange(N_COL, dtype=jnp.int32)[:, None]
            source = shaped[position, columns].astype(jnp.float32)
            weight = tile_map[row_number].astype(jnp.float32)
            source = source * weight[:, None, None, None]
            return jnp.einsum('kocs,cksw->ow', zrow, source)

        retarded = lax.map(row_field, jnp.arange(N_ROW, dtype=jnp.int32)).reshape(N, W)
        field = incident[instant] - retarded
        current = (load_gain[:, None] * field - load_cubic[:, None] * field * field * field).astype(jnp.bfloat16)
        buffer = buffer.at[H + instant].set(current)
        results.append(current)
    return jnp.stack(results)
```

```python
import functools

import jax
import jax.numpy as jnp
from jax import lax
from jax.experimental import pallas as pl
from jax.experimental.pallas import tpu as pltpu
from jax.sharding import PartitionSpec as P

BOTH = ("row", "col")
VMEM_BYTES = 48 * 1024 * 1024


def split_waves(waves):
    unit = 128
    if waves % unit or waves < 2 * unit:
        return [(0, waves)]
    half = (waves // unit + 1) // 2 * unit
    return [(0, half), (half, waves)]


def past_kernel(slots, depth, pieces, scalars, matrix, *refs):
    sources = refs[:pieces]
    incident, first_out, second_out, held, total, arrived = refs[pieces:]
    step = pl.program_id(0)
    waves = first_out.shape[1]
    share = incident.shape[1]

    def fetch(number, place):
        for which in range(pieces):
            @pl.when(number == which)
            def _():
                pltpu.make_async_copy(sources[which], held.at[place], arrived.at[place]).start()

    @pl.when(step == 0)
    def _():
        fetch(0, 0)
        total[...] = jnp.zeros_like(total)

    place = lax.rem(step, 2)

    @pl.when(step + 1 < pieces)
    def _():
        fetch(step + 1, 1 - place)

    pltpu.make_async_copy(sources[0], held.at[place], arrived.at[place]).wait()
    left = jnp.concatenate([matrix[slot] for slot in range(slots)], axis=1)
    right = []
    for slot in range(slots):
        delay = scalars[slot]
        now = held[place, depth - delay]
        later = held[place, jnp.minimum(depth + 1 - delay, depth - 1)]
        later = jnp.where(delay >= 2, later, jnp.zeros_like(later))
        right.append(jnp.concatenate([now, later], axis=1))
    right = jnp.concatenate(right, axis=0)
    total[...] += jnp.dot(left, right, preferred_element_type=jnp.float32)

    @pl.when(step == pieces - 1)
    def _():
        weight = -scalars[slots].astype(jnp.float32)
        first_out[...] = weight * total[:, :waves]
        second_out[...] = weight * total[:, waves:]
        own = pl.ds(pl.multiple_of(scalars[slots + 1], share), share)
        first_out[own, :] += incident[0]
        second_out[own, :] += incident[1]


def past_call(scalars, matrix, sources, incident):
    slots, rows, _ = matrix.shape
    depth, share_src, waves = sources[0].shape
    pieces = len(sources)
    flops = 2 * slots * rows * share_src * pieces * waves * 2
    return pl.pallas_call(
        functools.partial(past_kernel, slots, depth, pieces),
        out_shape=[jax.ShapeDtypeStruct((rows, waves), jnp.float32)] * 2,
        grid_spec=pltpu.PrefetchScalarGridSpec(
            num_scalar_prefetch=1,
            grid=(pieces,),
            in_specs=[pl.BlockSpec((slots, rows, share_src), lambda step, held: (0, 0, held[slots + 2 + step]))]
            + [pl.BlockSpec(memory_space=pl.ANY)] * pieces
            + [pl.BlockSpec(incident.shape, lambda step, held: (0, 0, 0))],
            out_specs=[pl.BlockSpec((rows, waves), lambda step, held: (0, 0))] * 2,
            scratch_shapes=[
                pltpu.VMEM((2, depth, share_src, waves), jnp.bfloat16),
                pltpu.VMEM((rows, 2 * waves), jnp.float32),
                pltpu.SemaphoreType.DMA((2,)),
            ],
        ),
        compiler_params=pltpu.CompilerParams(vmem_limit_bytes=VMEM_BYTES),
        cost_estimate=pl.CostEstimate(
            flops=flops, bytes_accessed=2 * slots * rows * share_src * pieces, transcendentals=0
        ),
    )(scalars, matrix, *sources, incident)


def recent_kernel(slots, parts, cols_count, scalars, matrix, *refs):
    sources = refs[:parts]
    base, kept_out, sent_out, total = refs[parts:]
    part, turn = pl.program_id(0), pl.program_id(1)
    used = scalars[slots]
    share = kept_out.shape[1]

    @pl.when((part == 0) & (turn == 0))
    def _():
        total[...] = jnp.zeros_like(total)

    for which in range(parts):
        @pl.when((part == which) & (turn < used))
        def _():
            total[...] += jnp.dot(matrix[0], sources[which][...], preferred_element_type=jnp.float32)

    @pl.when((part == parts - 1) & (turn == slots - 1))
    def _():
        weight = -scalars[slots + 1].astype(jnp.float32)
        bit = scalars[slots + 2]
        for pair in range(cols_count // 2):
            for out, own in ((kept_out, bit), (sent_out, 1 - bit)):
                rows = pl.ds(pl.multiple_of((2 * pair + own) * share, share), share)
                out[pair] = base[rows, :] + weight * total[rows, :]


def recent_call(scalars, matrix, sources, base, cols_count):
    slots, rows, _ = matrix.shape
    waves = base.shape[1]
    parts = len(sources)
    depth = sources[0].shape[0]
    share = rows // cols_count
    shape = (cols_count // 2, share, waves)
    whole = lambda part, turn, held: (0, 0)
    return pl.pallas_call(
        functools.partial(recent_kernel, slots, parts, cols_count),
        out_shape=[jax.ShapeDtypeStruct(shape, jnp.float32)] * 2,
        grid_spec=pltpu.PrefetchScalarGridSpec(
            num_scalar_prefetch=1,
            grid=(parts, slots),
            in_specs=[
                pl.BlockSpec(
                    (1, rows, depth), lambda part, turn, held: (held[turn], 0, held[slots + 3 + part])
                )
            ]
            + [pl.BlockSpec((depth, waves), whole)] * parts
            + [pl.BlockSpec((rows, waves), whole)],
            out_specs=[pl.BlockSpec(shape, lambda part, turn, held: (0, 0, 0))] * 2,
            scratch_shapes=[pltpu.VMEM((rows, waves), jnp.float32)],
        ),
        compiler_params=pltpu.CompilerParams(vmem_limit_bytes=VMEM_BYTES),
        cost_estimate=pl.CostEstimate(
            flops=2 * slots * rows * depth * parts * waves,
            bytes_accessed=2 * slots * rows * depth * parts,
            transcendentals=0,
        ),
    )(scalars, matrix, *sources, base)


def per_device(rows_count, cols_count, interaction, history, incident, load_gain, load_cubic, delays, tile_map):
    fanout = rows_count // cols_count
    layers = cols_count
    row_index, col_index = lax.axis_index("row"), lax.axis_index("col")
    layer, lane = row_index // fanout, row_index % fanout
    slots, block_obs, _ = interaction.shape
    share = incident.shape[1]
    delay = delays[0, 0]
    weight = tile_map[0, 0]
    bits = [1 << bit for bit in range((cols_count - 1).bit_length())]

    def send(value, target):
        pairs = []
        for row in range(rows_count):
            for col in range(cols_count):
                goal = target(row // fanout, row % fanout, col)
                if goal is not None:
                    pairs.append((row * cols_count + col, (goal[0] * fanout + goal[1]) * cols_count + goal[2]))
        return lax.ppermute(value, BOTH, pairs)

    def along_layers(value):
        return send(value, lambda layer, lane, col: ((layer - 1) % layers, lane, col))

    def along_lanes(value, steps):
        return send(value, lambda layer, lane, col: (layer, (lane - steps) % fanout, col))

    places = jnp.stack(
        [
            (layer + ahead) % layers * fanout + (lane + beside) % fanout
            for ahead in range(layers)
            for beside in range(fanout)
        ]
    )

    def in_row_order(values):
        rows = jnp.arange(rows_count, dtype=jnp.int32)
        held = (rows // fanout - layer) % layers * fanout + (rows % fanout - lane) % fanout
        ordered = jnp.take(jnp.stack(values), held, axis=0)
        return jnp.moveaxis(ordered, 0, 1).reshape(values[0].shape[0], -1, values[0].shape[2])

    if history.shape[1] % 128:
        places = jnp.zeros_like(places)
    past_scalars = jnp.concatenate([delay, jnp.stack([weight, col_index * share]), places]).astype(jnp.int32)
    recent = delay == 1
    order = jnp.argsort(jnp.where(recent, 0, 1), stable=True)
    used = jnp.sum(recent)
    order = order[jnp.minimum(jnp.arange(slots), jnp.maximum(used - 1, 0))]
    lanes_order = jnp.stack([(lane + beside) % fanout for beside in range(fanout)])
    recent_scalars = jnp.concatenate(
        [order, jnp.stack([used, weight, col_index % 2]), lanes_order]
    ).astype(jnp.int32)

    results = []
    for start, stop in split_waves(history.shape[2]):
        moving = history[:, :, start:stop]
        sources = []
        for ahead in range(layers):
            if ahead:
                moving = along_layers(moving)
            sources.append(moving)
            for beside in range(1, fanout):
                sources.append(along_lanes(moving, beside))
        if sources[0].shape[1] % 128:
            sources = [in_row_order(sources)]
        summands, later = past_call(past_scalars, interaction, sources, incident[:, :, start:stop])
        for bit in bits:
            summands = summands + send(
                summands,
                lambda layer, lane, col: (layer, lane, col ^ bit) if (layer ^ col) & (2 * bit - 1) == bit else None,
            )
        current = load_gain[:, None] * summands - load_cubic[:, None] * summands * summands * summands
        current = jnp.where(layer == col_index, current, 0.0).astype(jnp.bfloat16)

        scattered = current.reshape(cols_count, share, stop - start)
        for bit in reversed(bits):
            halves = scattered.reshape(2, bit, share, stop - start)
            own = (col_index // bit) % 2
            moved = send(
                lax.dynamic_index_in_dim(halves, 1 - own, 0, keepdims=False),
                lambda layer, lane, col: (layer, lane, col ^ bit) if (layer ^ col) & (2 * bit - 1) == 0 else None,
            )
            scattered = lax.dynamic_index_in_dim(halves, own, 0, keepdims=False) + moved

        for bit in reversed(bits):
            current = current + send(
                current,
                lambda layer, lane, col: (layer ^ bit, lane, col) if (layer ^ col) & (2 * bit - 1) == 0 else None,
            )
        sources = [current] + [along_lanes(current, beside) for beside in range(1, fanout)]
        kept, sent = recent_call(recent_scalars, interaction, sources, later, cols_count)
        for bit in bits:
            total = kept + send(sent, lambda layer, lane, col: (layer, lane, col ^ bit))
            if 2 * bit < cols_count:
                pairs = total.reshape(total.shape[0] // 2, 2, share, stop - start)
                own = (col_index // (2 * bit)) % 2
                kept = lax.dynamic_index_in_dim(pairs, own, 1, keepdims=False)
                sent = lax.dynamic_index_in_dim(pairs, 1 - own, 1, keepdims=False)
        field = total[0]
        gain = lax.dynamic_slice_in_dim(load_gain, col_index * share, share, 0)[:, None]
        cubic = lax.dynamic_slice_in_dim(load_cubic, col_index * share, share, 0)[:, None]
        last = (gain * field - cubic * field * field * field).astype(jnp.bfloat16)
        results.append(jnp.stack([scattered[0], last]))
    return jnp.concatenate(results, axis=2)


def solution(mesh):
    placed = (
        P(None, "row", "col"),
        P(None, ("col", "row"), None),
        P(None, ("row", "col"), None),
        P("row"),
        P("row"),
        P("row", "col", None),
        P("row", "col"),
    )
    return jax.shard_map(
        functools.partial(per_device, mesh.shape["row"], mesh.shape["col"]),
        mesh=mesh,
        in_specs=placed,
        out_specs=P(None, ("row", "col"), None),
        check_vma=False,
    )
```

```python
import functools

import jax
import jax.numpy as jnp
from jax import lax
from jax.experimental import pallas as pl
from jax.experimental.pallas import tpu as pltpu
from jax.sharding import PartitionSpec as P

BOTH = ("row", "col")
VMEM_BYTES = 8 * 1024 * 1024
TILE = 16
LANES = 128
LEVELS = 32000.0
IN_VMEM = pl.BlockSpec(memory_space=pltpu.VMEM)
IN_SMEM = pl.BlockSpec(memory_space=pltpu.SMEM)


def split_waves(waves):
    unit = 128
    if waves % unit or waves < 2 * unit:
        return [(0, waves)]
    half = (waves // unit + 1) // 2 * unit
    return [(0, half), (half, waves)]


def whereabouts(fanout):
    row = lax.axis_index("row")
    return lax.div(row, fanout), lax.rem(row, fanout), lax.axis_index("col")


def cycle_row(layers, fanout, place):
    lane, along = lax.div(place, layers), lax.rem(place, layers)
    return jnp.where(lax.rem(lane, 2) == 0, along, layers - 1 - along) * fanout + lane


def cycle_place(layers, layer, lane):
    return lane * layers + jnp.where(lax.rem(lane, 2) == 0, layer, layers - 1 - layer)


def first_kernel(matrix, gain, cubic, mark, own_gain, own_cubic, held):
    mark[...] = matrix[0, :8, :128].astype(jnp.float32)
    share = own_gain.shape[0]
    own = pl.ds(pl.multiple_of(lax.axis_index("col") * share, share), share)
    for source, out in ((gain, own_gain), (cubic, own_cubic)):
        for number in range(source.shape[0]):
            line = jnp.broadcast_to(source[number : number + 1, :], (LANES, LANES))
            held[number * LANES : (number + 1) * LANES, :] = jnp.transpose(line)
        out[...] = held[own, :]


def first_call(matrix, gain, cubic, share):
    rows = matrix.shape[1]
    lines = (rows // LANES, LANES)
    return pl.pallas_call(
        first_kernel,
        out_shape=[jax.ShapeDtypeStruct((8, LANES), jnp.float32)]
        + [jax.ShapeDtypeStruct((share, LANES), jnp.float32)] * 2,
        in_specs=[IN_VMEM] * 3,
        out_specs=[IN_VMEM] * 3,
        scratch_shapes=[pltpu.VMEM((rows, LANES), jnp.float32)],
        compiler_params=pltpu.CompilerParams(vmem_limit_bytes=VMEM_BYTES),
        cost_estimate=pl.CostEstimate(flops=0, bytes_accessed=4096, transcendentals=0),
    )(matrix, gain.reshape(lines), cubic.reshape(lines))


def past_kernel(number, opening, closing, layers, fanout, delays, tile, matrix, front, back, mark, *refs):
    refs = list(refs)
    carried = None if opening else refs.pop(0)
    incident = refs.pop(0) if closing else None
    slots = matrix.shape[0]
    depth, half, waves = front.shape
    layer, lane, col = whereabouts(fanout)
    count = matrix.shape[2] // (2 * half)
    here = cycle_place(layers, layer, lane)
    left, right = [], []
    for side, piece in enumerate((front, back)):
        if count == 1:
            place = side
        else:
            walked = lax.rem(here + (number if side else count - number), count)
            place = 2 * cycle_row(layers, fanout, walked) + side
        columns = pl.ds(pl.multiple_of(place * half, half), half)
        for slot in range(slots):
            delay = delays[slot]
            now = piece[depth - delay]
            later = piece[jnp.minimum(depth + 1 - delay, depth - 1)]
            later = jnp.where(delay >= 2, later, jnp.zeros_like(later))
            right.append(jnp.concatenate([now, later], axis=1))
            left.append(matrix[slot, :, columns])
    left, right = jnp.concatenate(left, axis=1), jnp.concatenate(right, axis=0)
    total = jnp.dot(left, right, preferred_element_type=jnp.float32)
    if not opening:
        total = total + carried[...]
    if not closing:
        refs[0][...] = total
        refs[1][...] = jnp.zeros_like(refs[1])
        return
    kept, sent, later, held = refs
    held[...] = -tile[0].astype(jnp.float32) * total
    share = incident.shape[1]
    own = pl.ds(pl.multiple_of(col * share, share), share)
    later[...] = held[:, waves:]
    later[own, :] += incident[1]
    bit = lax.rem(col, 2)
    for pair in range(kept.shape[0]):
        for out, which in ((kept, bit), (sent, 1 - bit)):
            rows = pl.ds(pl.multiple_of((2 * pair + which) * share, share), share)
            out[pair] = held[rows, :waves]
    kept[lax.div(col, 2)] += incident[0]


def past_call(delays, tile, matrix, pieces, mark, carried, incident, number, layers, fanout):
    slots, rows, _ = matrix.shape
    _, half, waves = pieces[0].shape
    totals = jax.ShapeDtypeStruct((rows, 2 * waves), jnp.float32)
    operands = [delays, tile, matrix, *pieces, mark]
    aliases, scratch = {}, []
    if carried is not None:
        operands.append(carried)
    if incident is None:
        ends = [totals, jax.ShapeDtypeStruct((8, 128), jnp.float32)]
        aliases = {} if carried is None else {6: 0}
    else:
        operands.append(incident)
        share = incident.shape[1]
        ends = [jax.ShapeDtypeStruct((rows // share // 2, share, waves), jnp.float32)] * 2
        ends.append(jax.ShapeDtypeStruct((rows, waves), jnp.float32))
        scratch = [pltpu.VMEM(totals.shape, jnp.float32)]
    return pl.pallas_call(
        functools.partial(past_kernel, number, carried is None, incident is not None, layers, fanout),
        out_shape=ends,
        in_specs=[IN_SMEM] * 2 + [IN_VMEM] * (len(operands) - 2),
        out_specs=[IN_VMEM] * len(ends),
        scratch_shapes=scratch,
        input_output_aliases=aliases,
        compiler_params=pltpu.CompilerParams(vmem_limit_bytes=VMEM_BYTES),
        cost_estimate=pl.CostEstimate(
            flops=8 * slots * rows * half * waves, bytes_accessed=4 * slots * rows * half, transcendentals=0
        ),
    )(*operands)


def small_call(kernel, shapes, matrix, *operands):
    return pl.pallas_call(
        kernel,
        out_shape=shapes,
        in_specs=[IN_VMEM] * (1 + len(operands)),
        out_specs=[IN_VMEM] * len(shapes),
        compiler_params=pltpu.CompilerParams(vmem_limit_bytes=VMEM_BYTES),
        cost_estimate=pl.CostEstimate(flops=0, bytes_accessed=1 << 20, transcendentals=0),
    )(matrix, *operands)


def fold_kernel(bit, last, matrix, kept, got, kept_out, sent_out):
    own = lax.rem(lax.div(lax.axis_index("col"), bit), 2)
    for pair in range(kept_out.shape[0]):
        kept_out[pair] = kept[2 * pair + own] + got[2 * pair + own]
        sent = kept[2 * pair + 1 - own] + got[2 * pair + 1 - own]
        if not last:
            sent_out[pair] = sent
            continue
        rows = sent.shape[0]
        peak = jnp.maximum(jnp.max(jnp.abs(sent), axis=0, keepdims=True), 1e-30)
        power = jnp.ceil(jnp.log2(peak))
        coded = jnp.round(sent * (jnp.exp2(-power) * LEVELS))
        sent_out[:rows] = coded.astype(jnp.int32).astype(jnp.int16)
        sent_out[rows:] = jnp.broadcast_to(power, (TILE, sent.shape[1])).astype(jnp.int32).astype(jnp.int16)


def fold_call(matrix, kept, got, bit, last):
    pairs, (share, waves) = kept.shape[0] // 2, kept.shape[1:]
    shapes = [jax.ShapeDtypeStruct((pairs, share, waves), jnp.float32)]
    if last:
        shapes.append(jax.ShapeDtypeStruct((share + TILE, waves), jnp.int16))
    else:
        shapes.append(shapes[0])
    return small_call(functools.partial(fold_kernel, bit, last), shapes, matrix, kept, got)


def load_kernel(matrix, kept, got, gain, cubic, out):
    share, waves = out.shape
    gain, cubic = (jnp.concatenate([ref[...]] * (waves // LANES), axis=1) for ref in (gain, cubic))
    power = got[share:].astype(jnp.int32).astype(jnp.float32)[:1]
    field = kept[0] + got[:share].astype(jnp.int32).astype(jnp.float32) * (jnp.exp2(power) * (1.0 / LEVELS))
    out[...] = (gain * field - cubic * field * field * field).astype(jnp.bfloat16)


def load_call(matrix, kept, got, gain, cubic):
    shapes = [jax.ShapeDtypeStruct(kept.shape[1:], jnp.bfloat16)]
    return small_call(load_kernel, shapes, matrix, kept, got, gain, cubic)[0]


def arrange_kernel(layers, fanout, matrix, *refs):
    layer, _, col = whereabouts(fanout)
    apart = layer ^ col
    for place in range(layers):
        @pl.when(apart == place)
        def _():
            for other in range(layers):
                refs[layers + other][...] = refs[place ^ other][...]


def arrange_call(matrix, values, fanout):
    shapes = [jax.ShapeDtypeStruct(value.shape, value.dtype) for value in values]
    return small_call(functools.partial(arrange_kernel, len(values), fanout), shapes, matrix, *values)


def recent_kernel(fanout, cols_count, delays, tile, matrix, *refs):
    sources = refs[: fanout * cols_count]
    base, kept, sent, held, total = refs[fanout * cols_count :]
    slots = matrix.shape[0]
    share = sources[0].shape[0]
    _, lane, col = whereabouts(fanout)
    for beside in range(fanout):
        for other in range(cols_count):
            place = lax.rem(lane + beside, fanout) * cols_count + (col ^ other)
            held[pl.ds(pl.multiple_of(place * share, share), share), :] = sources[beside * cols_count + other][...]
    total[...] = jnp.zeros_like(total)
    for slot in range(slots):
        @pl.when(delays[slot] == 1)
        def _():
            total[...] += jnp.dot(matrix[slot], held[...], preferred_element_type=jnp.float32)

    weight = -tile[0].astype(jnp.float32)
    bit = lax.rem(col, 2)
    for pair in range(cols_count // 2):
        for out, own in ((kept, bit), (sent, 1 - bit)):
            rows = pl.ds(pl.multiple_of((2 * pair + own) * share, share), share)
            out[pair] = base[rows, :] + weight * total[rows, :]


def recent_call(delays, tile, matrix, sources, base, fanout, cols_count):
    slots, rows, depth = matrix.shape
    share, waves = sources[0].shape
    return pl.pallas_call(
        functools.partial(recent_kernel, fanout, cols_count),
        out_shape=[jax.ShapeDtypeStruct((rows // share // 2, share, waves), jnp.float32)] * 2,
        in_specs=[IN_SMEM] * 2 + [IN_VMEM] * (len(sources) + 2),
        out_specs=[IN_VMEM] * 2,
        scratch_shapes=[pltpu.VMEM((depth, waves), jnp.bfloat16), pltpu.VMEM((rows, waves), jnp.float32)],
        compiler_params=pltpu.CompilerParams(vmem_limit_bytes=VMEM_BYTES),
        cost_estimate=pl.CostEstimate(
            flops=2 * slots * rows * depth * waves, bytes_accessed=2 * slots * rows * depth, transcendentals=0
        ),
    )(delays, tile, matrix, *sources, base)


def per_device(rows_count, cols_count, interaction, history, incident, load_gain, load_cubic, delays, tile_map):
    fanout = rows_count // cols_count
    layers = cols_count
    share = incident.shape[1]
    delay, tile = delays.reshape(-1), tile_map.reshape(-1)
    bits = [1 << bit for bit in range((cols_count - 1).bit_length())]

    def send(value, target):
        pairs = []
        for row in range(rows_count):
            for col in range(cols_count):
                goal = target(row // fanout, row % fanout, col)
                if goal is not None:
                    pairs.append((row * cols_count + col, (goal[0] * fanout + goal[1]) * cols_count + goal[2]))
        return lax.ppermute(value, BOTH, pairs)

    cycle = [
        (layer if lane % 2 == 0 else layers - 1 - layer) * fanout + lane
        for lane in range(fanout)
        for layer in range(layers)
    ]
    spot = {row: place for place, row in enumerate(cycle)}

    def around(value, steps):
        pairs = [(row, cycle[(spot[row] + steps) % rows_count]) for row in range(rows_count)]
        return lax.ppermute(value, "row", pairs)

    aligned = history.shape[1] % 256 == 0

    def in_row_order(values, sense):
        row = lax.axis_index("row")
        here = jnp.asarray([spot[row] for row in range(rows_count)], jnp.int32)[row]
        rows = jnp.asarray(cycle, jnp.int32)[(here - sense * jnp.arange(rows_count)) % rows_count]
        return jnp.take(jnp.stack(values), jnp.argsort(rows), axis=0)

    mark, gain, cubic = first_call(interaction, load_gain, load_cubic, share)

    def summed_and_loaded(kept, sent):
        for bit in bits:
            got = send(sent, lambda layer, lane, col: (layer, lane, col ^ bit))
            if bit != bits[-1]:
                kept, sent = fold_call(interaction, kept, got, 2 * bit, 2 * bit == bits[-1])
        return load_call(interaction, kept, got, gain, cubic)

    def to_layers(current, earlier):
        by_layer = {0: current}
        for bit in bits:
            for apart in list(by_layer):
                if apart == 0 and bit == 1 and earlier is not None:
                    by_layer[0], earlier[1] = lax.optimization_barrier((by_layer[0], earlier[1]))
                by_layer[apart ^ bit] = send(by_layer[apart], lambda layer, lane, col: (layer ^ bit, lane, col))
        return by_layer

    def to_sources(by_layer):
        ordered = arrange_call(interaction, [by_layer[apart] for apart in range(layers)], fanout)
        sources = {}
        for beside in reversed(range(fanout)):
            for other in range(cols_count):
                value = ordered[other]
                if beside or other:
                    value = send(
                        value, lambda layer, lane, col: (layer, (lane - beside) % fanout, col ^ other)
                    )
                sources[beside, other] = value
        return [sources[beside, other] for beside in range(fanout) for other in range(cols_count)]

    chunks = split_waves(history.shape[2])
    half = history.shape[1] // 2
    moving = [(history[:, :half, start:stop], history[:, half:, start:stop]) for start, stop in chunks]
    carried, marks = [None] * len(chunks), [None] * len(chunks)
    arrived = [[moving[number]] for number in range(len(chunks))]

    def add_piece(number, step):
        start, stop = chunks[number]
        ending = incident[:, :, start:stop] if step == rows_count - 1 else None
        outs = past_call(
            delay,
            tile,
            interaction,
            arrived[number][step],
            marks[number],
            carried[number],
            ending,
            step,
            layers,
            fanout,
        )
        carried[number], marks[number] = (outs[0], outs[1]) if ending is None else (outs, None)

    marks = [mark] * len(chunks)
    added = [0] * len(chunks)
    for step in range(1, rows_count):
        for number in range(len(chunks)):
            front, back = arrived[number][-1]
            if step >= 2 and aligned:
                wanted = 0 if step == 2 else 1 if step == 3 else step - 1
                while added[number] < wanted:
                    add_piece(number, added[number])
                    added[number] += 1
                front, back, marks[number] = lax.optimization_barrier((front, back, marks[number]))
            arrived[number].append((around(front, 1), around(back, -1)))
    if aligned:
        for step in range(rows_count):
            for number in range(len(chunks)):
                if step >= added[number]:
                    add_piece(number, step)
    if not aligned:
        for number, (start, stop) in enumerate(chunks):
            fronts, backs = zip(*arrived[number])
            ordered = jnp.stack([in_row_order(fronts, 1), in_row_order(backs, -1)], axis=1)
            ordered = jnp.moveaxis(ordered, 2, 0).reshape(history.shape[0], 2, rows_count * half, stop - start)
            pieces = ordered[:, 0], ordered[:, 1]
            ending = incident[:, :, start:stop]
            carried[number] = past_call(
                delay, tile, interaction, pieces, marks[number], None, ending, 0, layers, fanout
            )
    by_layers, results = [], []
    for kept, sent, _ in carried:
        current = summed_and_loaded(kept, sent)
        by_layers.append(to_layers(current, by_layers[-1] if by_layers else None))
    for by_layer, (_, _, later) in zip(by_layers, carried):
        kept, sent = recent_call(delay, tile, interaction, to_sources(by_layer), later, fanout, cols_count)
        results.append(jnp.stack([by_layer[0], summed_and_loaded(kept, sent)]))
    return jnp.concatenate(results, axis=2)


def solution(mesh):
    placed = (
        P(None, "row", "col"),
        P(None, ("col", "row"), None),
        P(None, ("row", "col"), None),
        P("row"),
        P("row"),
        P("row", "col", None),
        P("row", "col"),
    )
    return jax.shard_map(
        functools.partial(per_device, mesh.shape["row"], mesh.shape["col"]),
        mesh=mesh,
        in_specs=placed,
        out_specs=P(None, ("row", "col"), None),
        check_vma=False,
    )
```

```python
import functools

import jax
import jax.numpy as jnp
from jax import lax
from jax.experimental import pallas as pl
from jax.experimental.pallas import tpu as pltpu
from jax.sharding import PartitionSpec as P

BOTH = ("row", "col")
VMEM_BYTES = 8 * 1024 * 1024
TILE = 16
SHORT = pl.CostEstimate(flops=0, bytes_accessed=0, transcendentals=0)
LANES = 128
LEVELS = 32000.0
IN_VMEM = pl.BlockSpec(memory_space=pltpu.VMEM)
IN_SMEM = pl.BlockSpec(memory_space=pltpu.SMEM)


def split_waves(waves):
    unit = 128
    if waves % unit or waves < 2 * unit:
        return [(0, waves)]
    half = (waves // unit + 1) // 2 * unit
    return [(0, half), (half, waves)]


def whereabouts(fanout):
    row = lax.axis_index("row")
    return lax.div(row, fanout), lax.rem(row, fanout), lax.axis_index("col")


def cycle_row(layers, fanout, place):
    lane, along = lax.div(place, layers), lax.rem(place, layers)
    return jnp.where(lax.rem(lane, 2) == 0, along, layers - 1 - along) * fanout + lane


def cycle_place(layers, layer, lane):
    return lane * layers + jnp.where(lax.rem(lane, 2) == 0, layer, layers - 1 - layer)


def first_kernel(matrix, gain, cubic, mark, own_gain, own_cubic, held):
    mark[...] = matrix[0, :8, :128].astype(jnp.float32)
    share = own_gain.shape[0]
    own = pl.ds(pl.multiple_of(lax.axis_index("col") * share, share), share)
    for source, out in ((gain, own_gain), (cubic, own_cubic)):
        for number in range(source.shape[0]):
            line = jnp.broadcast_to(source[number : number + 1, :], (LANES, LANES))
            held[number * LANES : (number + 1) * LANES, :] = jnp.transpose(line)
        out[...] = held[own, :]


def first_call(matrix, gain, cubic, share):
    rows = matrix.shape[1]
    lines = (rows // LANES, LANES)
    return pl.pallas_call(
        first_kernel,
        out_shape=[jax.ShapeDtypeStruct((8, LANES), jnp.float32)]
        + [jax.ShapeDtypeStruct((share, LANES), jnp.float32)] * 2,
        in_specs=[IN_VMEM] * 3,
        out_specs=[IN_VMEM] * 3,
        scratch_shapes=[pltpu.VMEM((rows, LANES), jnp.float32)],
        compiler_params=pltpu.CompilerParams(vmem_limit_bytes=VMEM_BYTES),
        cost_estimate=SHORT,
    )(matrix, gain.reshape(lines), cubic.reshape(lines))


def past_kernel(number, opening, steps, layers, fanout, delays, tile, matrix, front, back, mark, *refs):
    refs = list(refs)
    carried = None if opening else refs.pop(0)
    incident = refs.pop(0) if len(steps) == 1 else None
    slots = matrix.shape[0]
    depth, half, waves = front.shape
    layer, lane, col = whereabouts(fanout)
    count = matrix.shape[2] // (2 * half)
    here = cycle_place(layers, layer, lane)
    left, right = [], []
    for side, piece in enumerate((front, back)):
        if count == 1:
            place = side
        else:
            walked = lax.rem(here + (number if side else count - number), count)
            place = 2 * cycle_row(layers, fanout, walked) + side
        columns = pl.ds(pl.multiple_of(place * half, half), half)
        for slot in range(slots):
            delay = delays[slot]
            parts = []
            if 0 in steps:
                parts.append(piece[depth - delay])
            if 1 in steps:
                later = piece[jnp.minimum(depth + 1 - delay, depth - 1)]
                parts.append(jnp.where(delay >= 2, later, jnp.zeros_like(later)))
            right.append(jnp.concatenate(parts, axis=1))
            left.append(matrix[slot, :, columns])
    left, right = jnp.concatenate(left, axis=1), jnp.concatenate(right, axis=0)
    total = jnp.dot(left, right, preferred_element_type=jnp.float32)
    if len(steps) == 2:
        refs[0][...] = total if opening else total + carried[...]
        refs[1][...] = jnp.zeros_like(refs[1])
        return
    if not opening:
        total = total + carried[:, steps[0] * waves : (steps[0] + 1) * waves]
    total = -tile[0].astype(jnp.float32) * total
    share = incident.shape[1]
    if steps[0]:
        refs[0][...] = total
        refs[0][pl.ds(pl.multiple_of(col * share, share), share), :] += incident[1]
        return
    kept, sent, held = refs
    held[...] = total
    bit = lax.rem(col, 2)
    for pair in range(kept.shape[0]):
        for out, which in ((kept, bit), (sent, 1 - bit)):
            rows = pl.ds(pl.multiple_of((2 * pair + which) * share, share), share)
            out[pair] = held[rows, :]
    kept[lax.div(col, 2)] += incident[0]


def past_call(delays, tile, matrix, pieces, mark, carried, incident, number, steps, layers, fanout):
    slots, rows, _ = matrix.shape
    _, half, waves = pieces[0].shape
    totals = jax.ShapeDtypeStruct((rows, 2 * waves), jnp.float32)
    operands = [delays, tile, matrix, *pieces, mark]
    aliases, scratch = {}, []
    if carried is not None:
        operands.append(carried)
    if len(steps) == 2:
        ends = [totals, jax.ShapeDtypeStruct((8, LANES), jnp.float32)]
        aliases = {} if carried is None else {6: 0}
    else:
        operands.append(incident)
        share = incident.shape[1]
        if steps[0]:
            ends = [jax.ShapeDtypeStruct((rows, waves), jnp.float32)]
        else:
            ends = [jax.ShapeDtypeStruct((rows // share // 2, share, waves), jnp.float32)] * 2
            scratch = [pltpu.VMEM((rows, waves), jnp.float32)]
    return pl.pallas_call(
        functools.partial(past_kernel, number, carried is None, steps, layers, fanout),
        out_shape=ends,
        in_specs=[IN_SMEM] * 2 + [IN_VMEM] * (len(operands) - 2),
        out_specs=[IN_VMEM] * len(ends),
        scratch_shapes=scratch,
        input_output_aliases=aliases,
        compiler_params=pltpu.CompilerParams(vmem_limit_bytes=VMEM_BYTES),
        cost_estimate=pl.CostEstimate(
            flops=4 * slots * rows * half * waves * len(steps),
            bytes_accessed=4 * slots * rows * half,
            transcendentals=0,
        ),
    )(*operands)


def small_call(kernel, shapes, matrix, *operands):
    return pl.pallas_call(
        kernel,
        out_shape=shapes,
        in_specs=[IN_VMEM] * (1 + len(operands)),
        out_specs=[IN_VMEM] * len(shapes),
        compiler_params=pltpu.CompilerParams(vmem_limit_bytes=VMEM_BYTES),
        cost_estimate=SHORT,
    )(matrix, *operands)


def fold_kernel(bit, last, matrix, kept, got, kept_out, sent_out):
    own = lax.rem(lax.div(lax.axis_index("col"), bit), 2)
    for pair in range(kept_out.shape[0]):
        kept_out[pair] = kept[2 * pair + own] + got[2 * pair + own]
        sent = kept[2 * pair + 1 - own] + got[2 * pair + 1 - own]
        if not last:
            sent_out[pair] = sent
            continue
        rows = sent.shape[0]
        peak = jnp.maximum(jnp.max(jnp.abs(sent), axis=0, keepdims=True), 1e-30)
        power = jnp.ceil(jnp.log2(peak))
        coded = jnp.round(sent * (jnp.exp2(-power) * LEVELS))
        sent_out[:rows] = coded.astype(jnp.int32).astype(jnp.int16)
        sent_out[rows:] = jnp.broadcast_to(power, (TILE, sent.shape[1])).astype(jnp.int32).astype(jnp.int16)


def fold_call(matrix, kept, got, bit, last):
    pairs, (share, waves) = kept.shape[0] // 2, kept.shape[1:]
    shapes = [jax.ShapeDtypeStruct((pairs, share, waves), jnp.float32)]
    if last:
        shapes.append(jax.ShapeDtypeStruct((share + TILE, waves), jnp.int16))
    else:
        shapes.append(shapes[0])
    return small_call(functools.partial(fold_kernel, bit, last), shapes, matrix, kept, got)


def load_kernel(matrix, kept, got, gain, cubic, out):
    share, waves = out.shape
    gain, cubic = (jnp.concatenate([ref[...]] * (waves // LANES), axis=1) for ref in (gain, cubic))
    power = got[share:].astype(jnp.int32).astype(jnp.float32)[:1]
    field = kept[0] + got[:share].astype(jnp.int32).astype(jnp.float32) * (jnp.exp2(power) * (1.0 / LEVELS))
    out[...] = (gain * field - cubic * field * field * field).astype(jnp.bfloat16)


def load_call(matrix, kept, got, gain, cubic):
    shapes = [jax.ShapeDtypeStruct(kept.shape[1:], jnp.bfloat16)]
    return small_call(load_kernel, shapes, matrix, kept, got, gain, cubic)[0]


def finish_kernel(matrix, kept, got, gain, cubic, *refs):
    values, out = refs[:-1], refs[-1]
    waves = kept.shape[2]
    load_kernel(matrix, kept, got, gain, cubic, out.at[1, :, out.shape[2] - waves :])
    start = 0
    for number, value in enumerate(values):
        step = 1 if number >= (len(values) + 1) // 2 else 0
        if number == (len(values) + 1) // 2:
            start = 0
        out[step, :, start : start + value.shape[1]] = value[...]
        start += value.shape[1]


def finish_call(matrix, kept, got, gain, cubic, firsts, lasts):
    share = kept.shape[1]
    waves = sum(value.shape[1] for value in firsts)
    shapes = [jax.ShapeDtypeStruct((2, share, waves), jnp.bfloat16)]
    return small_call(finish_kernel, shapes, matrix, kept, got, gain, cubic, *firsts, *lasts)[0]


def arrange_kernel(layers, fanout, matrix, *refs):
    layer, _, col = whereabouts(fanout)
    apart = layer ^ col
    for place in range(layers):
        @pl.when(apart == place)
        def _():
            for other in range(layers):
                refs[layers + other][...] = refs[place ^ other][...]


def arrange_call(matrix, values, fanout):
    shapes = [jax.ShapeDtypeStruct(value.shape, value.dtype) for value in values]
    return small_call(functools.partial(arrange_kernel, len(values), fanout), shapes, matrix, *values)


def recent_kernel(fanout, beside, ending, pieces, delays, tile, matrix, *refs):
    sources, base, refs = refs[:pieces], refs[pieces], list(refs[pieces + 1 :])
    outs = [refs.pop(0) for _ in range(2 if ending else 1)]
    total, held = refs
    slots = matrix.shape[0]
    _, lane, col = whereabouts(fanout)
    depth, share = held.shape[0], sources[0].shape[0]
    for other, source in enumerate(sources):
        held[pl.ds(pl.multiple_of((col ^ other) * share, share), share), :] = source[...]
    lane = lax.rem(lane + beside, fanout)
    columns = pl.ds(pl.multiple_of(lane * depth, depth), depth)
    total[...] = jnp.zeros_like(total)
    for slot in range(slots):
        @pl.when(delays[slot] == 1)
        def _():
            total[...] += jnp.dot(matrix[slot, :, columns], held[...], preferred_element_type=jnp.float32)

    weight = -tile[0].astype(jnp.float32)
    if not ending:
        outs[0][...] = base[...] + weight * total[...]
        return
    bit = lax.rem(col, 2)
    for pair in range(outs[0].shape[0]):
        for out, own in ((outs[0], bit), (outs[1], 1 - bit)):
            rows = pl.ds(pl.multiple_of((2 * pair + own) * share, share), share)
            out[pair] = base[rows, :] + weight * total[rows, :]


def recent_call(delays, tile, matrix, sources, base, beside, fanout, cols_count):
    slots, rows, depth = matrix.shape
    waves = base.shape[1]
    depth = depth // fanout
    ending = beside == fanout - 1
    if ending:
        ends = [jax.ShapeDtypeStruct((cols_count // 2, rows // cols_count, waves), jnp.float32)] * 2
    else:
        ends = [jax.ShapeDtypeStruct(base.shape, jnp.float32)]
    return pl.pallas_call(
        functools.partial(recent_kernel, fanout, beside, ending, len(sources)),
        out_shape=ends,
        in_specs=[IN_SMEM] * 2 + [IN_VMEM] * (len(sources) + 2),
        out_specs=[IN_VMEM] * len(ends),
        scratch_shapes=[pltpu.VMEM((rows, waves), jnp.float32), pltpu.VMEM((depth, waves), jnp.bfloat16)],
        compiler_params=pltpu.CompilerParams(vmem_limit_bytes=VMEM_BYTES),
        cost_estimate=SHORT,
    )(delays, tile, matrix, *sources, base)


def per_device(rows_count, cols_count, interaction, history, incident, load_gain, load_cubic, delays, tile_map):
    fanout = rows_count // cols_count
    layers = cols_count
    share = incident.shape[1]
    delay, tile = delays.reshape(-1), tile_map.reshape(-1)
    bits = [1 << bit for bit in range((cols_count - 1).bit_length())]

    def send(value, target):
        pairs = []
        for row in range(rows_count):
            for col in range(cols_count):
                goal = target(row // fanout, row % fanout, col)
                if goal is not None:
                    pairs.append((row * cols_count + col, (goal[0] * fanout + goal[1]) * cols_count + goal[2]))
        return lax.ppermute(value, BOTH, pairs)

    cycle = [
        (layer if lane % 2 == 0 else layers - 1 - layer) * fanout + lane
        for lane in range(fanout)
        for layer in range(layers)
    ]
    spot = {row: place for place, row in enumerate(cycle)}

    def around(value, steps):
        pairs = [(row, cycle[(spot[row] + steps) % rows_count]) for row in range(rows_count)]
        return lax.ppermute(value, "row", pairs)

    aligned = history.shape[1] % 256 == 0

    def in_row_order(values, sense):
        row = lax.axis_index("row")
        here = jnp.asarray([spot[row] for row in range(rows_count)], jnp.int32)[row]
        rows = jnp.asarray(cycle, jnp.int32)[(here - sense * jnp.arange(rows_count)) % rows_count]
        return jnp.take(jnp.stack(values), jnp.argsort(rows), axis=0)

    mark, gain, cubic = first_call(interaction, load_gain, load_cubic, share)

    def folded(kept, sent):
        for bit in bits[:-1]:
            got = send(sent, lambda layer, lane, col: (layer, lane, col ^ bit))
            kept, sent = fold_call(interaction, kept, got, 2 * bit, 2 * bit == bits[-1])
        return kept, sent

    def last_hop(sent):
        return send(sent, lambda layer, lane, col: (layer, lane, col ^ bits[-1]))

    def to_layers(current):
        by_layer = {0: current}
        for bit in reversed(bits):
            for apart in list(by_layer):
                value = by_layer[apart]
                if apart and bit in by_layer:
                    value, by_layer[bit] = lax.optimization_barrier((value, by_layer[bit]))
                by_layer[apart ^ bit] = send(value, lambda layer, lane, col: (layer ^ bit, lane, col))
        return by_layer

    def to_sources(ordered):
        lanes = [None] * fanout
        for beside in reversed(range(fanout)):
            lanes[beside] = [
                send(ordered[other], lambda layer, lane, col: (layer, (lane - beside) % fanout, col ^ other))
                if beside or other
                else ordered[0]
                for other in range(cols_count)
            ]
        return lanes

    chunks = split_waves(history.shape[2])
    half = history.shape[1] // 2
    moving = [(history[:, :half, start:stop], history[:, half:, start:stop]) for start, stop in chunks]
    carried, marks = [None] * len(chunks), [None] * len(chunks)
    arrived = [[moving[number]] for number in range(len(chunks))]

    def add_piece(number, step):
        start, stop = chunks[number]
        outs = past_call(
            delay,
            tile,
            interaction,
            arrived[number][step],
            marks[number],
            carried[number],
            None,
            step,
            (0, 1),
            layers,
            fanout,
        )
        carried[number], marks[number] = outs

    marks = [mark] * len(chunks)
    added = [0] * len(chunks)
    for step in range(1, rows_count):
        for number in range(len(chunks)):
            front, back = arrived[number][-1]
            if step >= 2 and aligned:
                wanted = 0 if step == 2 else 1 if step == 3 else step - 1
                while added[number] < wanted:
                    add_piece(number, added[number])
                    added[number] += 1
                front, back, marks[number] = lax.optimization_barrier((front, back, marks[number]))
            arrived[number].append((around(front, 1), around(back, -1)))
    last = rows_count - 1
    for number, (start, stop) in enumerate(chunks):
        if aligned:
            for step in range(added[number], last):
                add_piece(number, step)
            arrived[number] = arrived[number][last]
        else:
            fronts, backs = zip(*arrived[number])
            ordered = jnp.stack([in_row_order(fronts, 1), in_row_order(backs, -1)], axis=1)
            ordered = jnp.moveaxis(ordered, 2, 0).reshape(history.shape[0], 2, rows_count * half, stop - start)
            arrived[number] = ordered[:, 0], ordered[:, 1]

    def end_past(number, step):
        start, stop = chunks[number]
        return past_call(
            delay,
            tile,
            interaction,
            arrived[number],
            marks[number],
            carried[number],
            incident[:, :, start:stop],
            last,
            (step,),
            layers,
            fanout,
        )

    numbers = range(len(chunks))
    kepts, sents = [None] * len(chunks), [None] * len(chunks)
    for number in numbers:
        kepts[number], sents[number] = folded(*end_past(number, 0))
    gots, laters = [], []
    for number in numbers:
        gots.append(last_hop(sents[number]))
        sents[number], marks[number] = lax.optimization_barrier((sents[number], marks[number]))
        later, gots[number] = lax.optimization_barrier((end_past(number, 1)[0], gots[number]))
        laters.append(later)
    by_layers = [to_layers(load_call(interaction, kepts[number], gots[number], gain, cubic)) for number in numbers]
    every, ends = [], []
    for number in numbers:
        ordered = arrange_call(interaction, [by_layers[number][apart] for apart in range(layers)], fanout)
        if number:
            ordered, ends[-1] = lax.optimization_barrier((ordered, ends[-1]))
        every.append(to_sources(ordered))
        ends.append(
            recent_call(delay, tile, interaction, every[number][0], laters[number], 0, fanout, cols_count)
        )
    for number in numbers:
        for beside in range(1, fanout):
            ends[number] = recent_call(
                delay, tile, interaction, every[number][beside], ends[number][0], beside, fanout, cols_count
            )
        kepts[number], sents[number] = folded(*ends[number])
    gots = [last_hop(sents[number]) for number in numbers]
    lasts = [load_call(interaction, kepts[number], gots[number], gain, cubic) for number in numbers[:-1]]
    firsts = [by_layer[0] for by_layer in by_layers]
    return finish_call(interaction, kepts[-1], gots[-1], gain, cubic, firsts, lasts)


def solution(mesh):
    placed = (
        P(None, "row", "col"),
        P(None, ("col", "row"), None),
        P(None, ("row", "col"), None),
        P("row"),
        P("row"),
        P("row", "col", None),
        P("row", "col"),
    )
    return jax.shard_map(
        functools.partial(per_device, mesh.shape["row"], mesh.shape["col"]),
        mesh=mesh,
        in_specs=placed,
        out_specs=P(None, ("row", "col"), None),
        check_vma=False,
    )
```

```python
import functools

import jax
import jax.numpy as jnp
from jax import lax
from jax.experimental import pallas as pl
from jax.experimental.pallas import tpu as pltpu
from jax.sharding import PartitionSpec as P

BOTH = ("row", "col")
VMEM_BYTES = 8 * 1024 * 1024
TILE = 16
SHORT = pl.CostEstimate(flops=0, bytes_accessed=0, transcendentals=0)
LANES = 128
LEVELS = 32000.0
IN_VMEM = pl.BlockSpec(memory_space=pltpu.VMEM)
IN_SMEM = pl.BlockSpec(memory_space=pltpu.SMEM)


def split_waves(waves):
    unit = 128
    if waves % unit or waves < 2 * unit:
        return [(0, waves)]
    half = (waves // unit + 1) // 2 * unit
    return [(0, half), (half, waves)]


def whereabouts(fanout):
    row = lax.axis_index("row")
    return lax.div(row, fanout), lax.rem(row, fanout), lax.axis_index("col")


def cycle_row(layers, fanout, place):
    lane, along = lax.div(place, layers), lax.rem(place, layers)
    return jnp.where(lax.rem(lane, 2) == 0, along, layers - 1 - along) * fanout + lane


def cycle_place(layers, layer, lane):
    return lane * layers + jnp.where(lax.rem(lane, 2) == 0, layer, layers - 1 - layer)


def first_kernel(matrix, gain, cubic, mark, own_gain, own_cubic, held):
    mark[...] = matrix[0, :8, :128].astype(jnp.float32)
    share = own_gain.shape[0]
    own = pl.ds(pl.multiple_of(lax.axis_index("col") * share, share), share)
    for source, out in ((gain, own_gain), (cubic, own_cubic)):
        for number in range(source.shape[0]):
            line = jnp.broadcast_to(source[number : number + 1, :], (LANES, LANES))
            held[number * LANES : (number + 1) * LANES, :] = jnp.transpose(line)
        out[...] = held[own, :]


def first_call(matrix, gain, cubic, share):
    rows = matrix.shape[1]
    lines = (rows // LANES, LANES)
    return pl.pallas_call(
        first_kernel,
        out_shape=[jax.ShapeDtypeStruct((8, LANES), jnp.float32)]
        + [jax.ShapeDtypeStruct((share, LANES), jnp.float32)] * 2,
        in_specs=[IN_VMEM] * 3,
        out_specs=[IN_VMEM] * 3,
        scratch_shapes=[pltpu.VMEM((rows, LANES), jnp.float32)],
        compiler_params=pltpu.CompilerParams(vmem_limit_bytes=VMEM_BYTES),
        cost_estimate=SHORT,
    )(matrix, gain.reshape(lines), cubic.reshape(lines))


def past_kernel(number, opening, steps, layers, fanout, delays, tile, matrix, front, back, mark, *refs):
    refs = list(refs)
    carried = None if opening else refs.pop(0)
    incident = refs.pop(0) if len(steps) == 1 else None
    slots = matrix.shape[0]
    depth, half, waves = front.shape
    layer, lane, col = whereabouts(fanout)
    count = matrix.shape[2] // (2 * half)
    here = cycle_place(layers, layer, lane)
    left, right = [], []
    for side, piece in enumerate((front, back)):
        if count == 1:
            place = side
        else:
            walked = lax.rem(here + (number if side else count - number), count)
            place = 2 * cycle_row(layers, fanout, walked) + side
        columns = pl.ds(pl.multiple_of(place * half, half), half)
        for slot in range(slots):
            delay = delays[slot]
            parts = []
            if 0 in steps:
                parts.append(piece[depth - delay])
            if 1 in steps:
                later = piece[jnp.minimum(depth + 1 - delay, depth - 1)]
                parts.append(jnp.where(delay >= 2, later, jnp.zeros_like(later)))
            right.append(jnp.concatenate(parts, axis=1))
            left.append(matrix[slot, :, columns])
    left, right = jnp.concatenate(left, axis=1), jnp.concatenate(right, axis=0)
    total = jnp.dot(left, right, preferred_element_type=jnp.float32)
    if len(steps) == 2:
        refs[0][...] = total if opening else total + carried[...]
        refs[1][...] = jnp.zeros_like(refs[1])
        return
    if not opening:
        total = total + carried[:, steps[0] * waves : (steps[0] + 1) * waves]
    total = -tile[0].astype(jnp.float32) * total
    share = incident.shape[1]
    if steps[0]:
        refs[0][...] = total
        refs[0][pl.ds(pl.multiple_of(col * share, share), share), :] += incident[1]
        return
    kept, sent, held = refs
    held[...] = total
    bit = lax.rem(col, 2)
    for pair in range(kept.shape[0]):
        for out, which in ((kept, bit), (sent, 1 - bit)):
            rows = pl.ds(pl.multiple_of((2 * pair + which) * share, share), share)
            out[pair] = held[rows, :]
    kept[lax.div(col, 2)] += incident[0]


def past_call(delays, tile, matrix, pieces, mark, carried, incident, number, steps, layers, fanout):
    slots, rows, _ = matrix.shape
    _, half, waves = pieces[0].shape
    totals = jax.ShapeDtypeStruct((rows, 2 * waves), jnp.float32)
    operands = [delays, tile, matrix, *pieces, mark]
    aliases, scratch = {}, []
    if carried is not None:
        operands.append(carried)
    if len(steps) == 2:
        ends = [totals, jax.ShapeDtypeStruct((8, LANES), jnp.float32)]
        aliases = {} if carried is None else {6: 0}
    else:
        operands.append(incident)
        share = incident.shape[1]
        if steps[0]:
            ends = [jax.ShapeDtypeStruct((rows, waves), jnp.float32)]
        else:
            ends = [jax.ShapeDtypeStruct((rows // share // 2, share, waves), jnp.float32)] * 2
            scratch = [pltpu.VMEM((rows, waves), jnp.float32)]
    return pl.pallas_call(
        functools.partial(past_kernel, number, carried is None, steps, layers, fanout),
        out_shape=ends,
        in_specs=[IN_SMEM] * 2 + [IN_VMEM] * (len(operands) - 2),
        out_specs=[IN_VMEM] * len(ends),
        scratch_shapes=scratch,
        input_output_aliases=aliases,
        compiler_params=pltpu.CompilerParams(vmem_limit_bytes=VMEM_BYTES),
        cost_estimate=pl.CostEstimate(
            flops=4 * slots * rows * half * waves * len(steps),
            bytes_accessed=4 * slots * rows * half,
            transcendentals=0,
        ),
    )(*operands)


def small_call(kernel, shapes, matrix, *operands):
    return pl.pallas_call(
        kernel,
        out_shape=shapes,
        in_specs=[IN_VMEM] * (1 + len(operands)),
        out_specs=[IN_VMEM] * len(shapes),
        compiler_params=pltpu.CompilerParams(vmem_limit_bytes=VMEM_BYTES),
        cost_estimate=SHORT,
    )(matrix, *operands)


def fold_kernel(bit, last, matrix, kept, got, kept_out, sent_out):
    own = lax.rem(lax.div(lax.axis_index("col"), bit), 2)
    for pair in range(kept_out.shape[0]):
        kept_out[pair] = kept[2 * pair + own] + got[2 * pair + own]
        sent = kept[2 * pair + 1 - own] + got[2 * pair + 1 - own]
        if not last:
            sent_out[pair] = sent
            continue
        rows = sent.shape[0]
        peak = jnp.maximum(jnp.max(jnp.abs(sent), axis=0, keepdims=True), 1e-30)
        power = jnp.ceil(jnp.log2(peak))
        coded = jnp.round(sent * (jnp.exp2(-power) * LEVELS))
        sent_out[:rows] = coded.astype(jnp.int32).astype(jnp.int16)
        sent_out[rows:] = jnp.broadcast_to(power, (TILE, sent.shape[1])).astype(jnp.int32).astype(jnp.int16)


def fold_call(matrix, kept, got, bit, last):
    pairs, (share, waves) = kept.shape[0] // 2, kept.shape[1:]
    shapes = [jax.ShapeDtypeStruct((pairs, share, waves), jnp.float32)]
    if last:
        shapes.append(jax.ShapeDtypeStruct((share + TILE, waves), jnp.int16))
    else:
        shapes.append(shapes[0])
    return small_call(functools.partial(fold_kernel, bit, last), shapes, matrix, kept, got)


def load_kernel(matrix, kept, got, gain, cubic, out):
    share, waves = out.shape
    gain, cubic = (jnp.concatenate([ref[...]] * (waves // LANES), axis=1) for ref in (gain, cubic))
    power = got[share:].astype(jnp.int32).astype(jnp.float32)[:1]
    field = kept[0] + got[:share].astype(jnp.int32).astype(jnp.float32) * (jnp.exp2(power) * (1.0 / LEVELS))
    out[...] = (gain * field - cubic * field * field * field).astype(jnp.bfloat16)


def load_call(matrix, kept, got, gain, cubic):
    shapes = [jax.ShapeDtypeStruct(kept.shape[1:], jnp.bfloat16)]
    return small_call(load_kernel, shapes, matrix, kept, got, gain, cubic)[0]


def finish_kernel(matrix, kept, got, gain, cubic, *refs):
    values, out = refs[:-1], refs[-1]
    waves = kept.shape[2]
    load_kernel(matrix, kept, got, gain, cubic, out.at[1, :, out.shape[2] - waves :])
    start = 0
    for number, value in enumerate(values):
        step = 1 if number >= (len(values) + 1) // 2 else 0
        if number == (len(values) + 1) // 2:
            start = 0
        out[step, :, start : start + value.shape[1]] = value[...]
        start += value.shape[1]


def finish_call(matrix, kept, got, gain, cubic, firsts, lasts):
    share = kept.shape[1]
    waves = sum(value.shape[1] for value in firsts)
    shapes = [jax.ShapeDtypeStruct((2, share, waves), jnp.bfloat16)]
    return small_call(finish_kernel, shapes, matrix, kept, got, gain, cubic, *firsts, *lasts)[0]


def arrange_kernel(layers, fanout, matrix, *refs):
    layer, _, col = whereabouts(fanout)
    apart = layer ^ col
    for place in range(layers):
        @pl.when(apart == place)
        def _():
            for other in range(layers):
                refs[layers + other][...] = refs[place ^ other][...]


def arrange_call(matrix, values, fanout):
    shapes = [jax.ShapeDtypeStruct(value.shape, value.dtype) for value in values]
    return small_call(functools.partial(arrange_kernel, len(values), fanout), shapes, matrix, *values)


def recent_kernel(fanout, beside, ending, pieces, delays, tile, matrix, *refs):
    sources, base, refs = refs[:pieces], refs[pieces], list(refs[pieces + 1 :])
    outs = [refs.pop(0) for _ in range(2 if ending else 1)]
    total, held = refs
    slots = matrix.shape[0]
    _, lane, col = whereabouts(fanout)
    depth, share = held.shape[0], sources[0].shape[0]
    for other, source in enumerate(sources):
        held[pl.ds(pl.multiple_of((col ^ other) * share, share), share), :] = source[...]
    lane = lax.rem(lane + beside, fanout)
    columns = pl.ds(pl.multiple_of(lane * depth, depth), depth)
    total[...] = jnp.zeros_like(total)
    for slot in range(slots):
        @pl.when(delays[slot] == 1)
        def _():
            total[...] += jnp.dot(matrix[slot, :, columns], held[...], preferred_element_type=jnp.float32)

    weight = -tile[0].astype(jnp.float32)
    if not ending:
        outs[0][...] = base[...] + weight * total[...]
        return
    bit = lax.rem(col, 2)
    for pair in range(outs[0].shape[0]):
        for out, own in ((outs[0], bit), (outs[1], 1 - bit)):
            rows = pl.ds(pl.multiple_of((2 * pair + own) * share, share), share)
            out[pair] = base[rows, :] + weight * total[rows, :]


def recent_call(delays, tile, matrix, sources, base, beside, fanout, cols_count):
    slots, rows, depth = matrix.shape
    waves = base.shape[1]
    depth = depth // fanout
    ending = beside == fanout - 1
    if ending:
        ends = [jax.ShapeDtypeStruct((cols_count // 2, rows // cols_count, waves), jnp.float32)] * 2
    else:
        ends = [jax.ShapeDtypeStruct(base.shape, jnp.float32)]
    return pl.pallas_call(
        functools.partial(recent_kernel, fanout, beside, ending, len(sources)),
        out_shape=ends,
        in_specs=[IN_SMEM] * 2 + [IN_VMEM] * (len(sources) + 2),
        out_specs=[IN_VMEM] * len(ends),
        scratch_shapes=[pltpu.VMEM((rows, waves), jnp.float32), pltpu.VMEM((depth, waves), jnp.bfloat16)],
        compiler_params=pltpu.CompilerParams(vmem_limit_bytes=VMEM_BYTES),
        cost_estimate=SHORT,
    )(delays, tile, matrix, *sources, base)


def per_device(rows_count, cols_count, interaction, history, incident, load_gain, load_cubic, delays, tile_map):
    fanout = rows_count // cols_count
    layers = cols_count
    share = incident.shape[1]
    delay, tile = delays.reshape(-1), tile_map.reshape(-1)
    bits = [1 << bit for bit in range((cols_count - 1).bit_length())]

    def send(value, target):
        pairs = []
        for row in range(rows_count):
            for col in range(cols_count):
                goal = target(row // fanout, row % fanout, col)
                if goal is not None:
                    pairs.append((row * cols_count + col, (goal[0] * fanout + goal[1]) * cols_count + goal[2]))
        return lax.ppermute(value, BOTH, pairs)

    cycle = [
        (layer if lane % 2 == 0 else layers - 1 - layer) * fanout + lane
        for lane in range(fanout)
        for layer in range(layers)
    ]
    spot = {row: place for place, row in enumerate(cycle)}

    def around(value, steps):
        pairs = [(row, cycle[(spot[row] + steps) % rows_count]) for row in range(rows_count)]
        return lax.ppermute(value, "row", pairs)

    aligned = history.shape[1] % 256 == 0

    def in_row_order(values, sense):
        row = lax.axis_index("row")
        here = jnp.asarray([spot[row] for row in range(rows_count)], jnp.int32)[row]
        rows = jnp.asarray(cycle, jnp.int32)[(here - sense * jnp.arange(rows_count)) % rows_count]
        return jnp.take(jnp.stack(values), jnp.argsort(rows), axis=0)

    mark, gain, cubic = first_call(interaction, load_gain, load_cubic, share)

    def folded(kept, sent):
        for bit in bits[:-1]:
            got = send(sent, lambda layer, lane, col: (layer, lane, col ^ bit))
            kept, sent = fold_call(interaction, kept, got, 2 * bit, 2 * bit == bits[-1])
        return kept, sent

    def last_hop(sent):
        return send(sent, lambda layer, lane, col: (layer, lane, col ^ bits[-1]))

    def to_layers(current):
        by_layer = {0: current}
        for bit in reversed(bits):
            for apart in list(by_layer):
                value = by_layer[apart]
                if apart and bit in by_layer:
                    value, by_layer[bit] = lax.optimization_barrier((value, by_layer[bit]))
                by_layer[apart ^ bit] = send(value, lambda layer, lane, col: (layer ^ bit, lane, col))
        return by_layer

    def to_sources(ordered):
        lanes = [None] * fanout
        for beside in reversed(range(fanout)):
            lanes[beside] = [
                send(ordered[other], lambda layer, lane, col: (layer, (lane - beside) % fanout, col ^ other))
                if beside or other
                else ordered[0]
                for other in range(cols_count)
            ]
        return lanes

    chunks = split_waves(history.shape[2])
    half = history.shape[1] // 2
    moving = [(history[:, :half, start:stop], history[:, half:, start:stop]) for start, stop in chunks]
    carried, marks = [None] * len(chunks), [None] * len(chunks)
    arrived = [[moving[number]] for number in range(len(chunks))]

    def add_piece(number, step):
        start, stop = chunks[number]
        outs = past_call(
            delay,
            tile,
            interaction,
            arrived[number][step],
            marks[number],
            carried[number],
            None,
            step,
            (0, 1),
            layers,
            fanout,
        )
        carried[number], marks[number] = outs

    marks = [mark] * len(chunks)
    added = [0] * len(chunks)
    for step in range(1, rows_count):
        for number in range(len(chunks)):
            front, back = arrived[number][-1]
            if step >= 2 and aligned:
                wanted = 0 if step == 2 else 1 if step == 3 else step - 1
                while added[number] < wanted:
                    add_piece(number, added[number])
                    added[number] += 1
                front, back, marks[number] = lax.optimization_barrier((front, back, marks[number]))
            arrived[number].append((around(front, 1), around(back, -1)))
    last = rows_count - 1
    for number, (start, stop) in enumerate(chunks):
        if aligned:
            for step in range(added[number], last):
                add_piece(number, step)
            arrived[number] = arrived[number][last]
        else:
            fronts, backs = zip(*arrived[number])
            ordered = jnp.stack([in_row_order(fronts, 1), in_row_order(backs, -1)], axis=1)
            ordered = jnp.moveaxis(ordered, 2, 0).reshape(history.shape[0], 2, rows_count * half, stop - start)
            arrived[number] = ordered[:, 0], ordered[:, 1]

    def end_past(number, step):
        start, stop = chunks[number]
        return past_call(
            delay,
            tile,
            interaction,
            arrived[number],
            marks[number],
            carried[number],
            incident[:, :, start:stop],
            last,
            (step,),
            layers,
            fanout,
        )

    numbers = range(len(chunks))
    kepts, sents = [None] * len(chunks), [None] * len(chunks)
    for number in numbers:
        kepts[number], sents[number] = folded(*end_past(number, 0))
    gots, laters = [], []
    for number in numbers:
        gots.append(last_hop(sents[number]))
        sents[number], marks[number] = lax.optimization_barrier((sents[number], marks[number]))
        laters.append(end_past(number, 1)[0])
    by_layers = [to_layers(load_call(interaction, kepts[number], gots[number], gain, cubic)) for number in numbers]
    every, ends = [], []
    for number in numbers:
        ordered = arrange_call(interaction, [by_layers[number][apart] for apart in range(layers)], fanout)
        if number:
            ordered, ends[-1] = lax.optimization_barrier((ordered, ends[-1]))
        every.append(to_sources(ordered))
        ends.append(
            recent_call(delay, tile, interaction, every[number][0], laters[number], 0, fanout, cols_count)
        )
    for number in numbers:
        for beside in range(1, fanout):
            ends[number] = recent_call(
                delay, tile, interaction, every[number][beside], ends[number][0], beside, fanout, cols_count
            )
        kepts[number], sents[number] = folded(*ends[number])
    gots = [last_hop(sents[number]) for number in numbers]
    lasts = [load_call(interaction, kepts[number], gots[number], gain, cubic) for number in numbers[:-1]]
    firsts = [by_layer[0] for by_layer in by_layers]
    return finish_call(interaction, kepts[-1], gots[-1], gain, cubic, firsts, lasts)


def solution(mesh):
    placed = (
        P(None, "row", "col"),
        P(None, ("col", "row"), None),
        P(None, ("row", "col"), None),
        P("row"),
        P("row"),
        P("row", "col", None),
        P("row", "col"),
    )
    return jax.shard_map(
        functools.partial(per_device, mesh.shape["row"], mesh.shape["col"]),
        mesh=mesh,
        in_specs=placed,
        out_specs=P(None, ("row", "col"), None),
        check_vma=False,
    )
```

```python
import functools

import jax
import jax.numpy as jnp
from jax import lax
from jax.experimental import pallas as pl
from jax.experimental.pallas import tpu as pltpu
from jax.sharding import PartitionSpec as P

BOTH = ("row", "col")
VMEM_BYTES = 8 * 1024 * 1024
TILE = 16
SHORT = pl.CostEstimate(flops=0, bytes_accessed=0, transcendentals=0)
LANES = 128
LEVELS = 32000.0
IN_VMEM = pl.BlockSpec(memory_space=pltpu.VMEM)
IN_SMEM = pl.BlockSpec(memory_space=pltpu.SMEM)


def split_waves(waves):
    unit = 128
    if waves % unit or waves < 2 * unit:
        return [(0, waves)]
    half = (waves // unit + 1) // 2 * unit
    return [(0, half), (half, waves)]


def whereabouts(fanout):
    row = lax.axis_index("row")
    return lax.div(row, fanout), lax.rem(row, fanout), lax.axis_index("col")


def cycle_row(layers, fanout, place):
    lane, along = lax.div(place, layers), lax.rem(place, layers)
    return jnp.where(lax.rem(lane, 2) == 0, along, layers - 1 - along) * fanout + lane


def cycle_place(layers, layer, lane):
    return lane * layers + jnp.where(lax.rem(lane, 2) == 0, layer, layers - 1 - layer)


def first_kernel(matrix, gain, cubic, mark, own_gain, own_cubic, held):
    mark[...] = matrix[0, :8, :128].astype(jnp.float32)
    share = own_gain.shape[0]
    own = pl.ds(pl.multiple_of(lax.axis_index("col") * share, share), share)
    for source, out in ((gain, own_gain), (cubic, own_cubic)):
        for number in range(source.shape[0]):
            line = jnp.broadcast_to(source[number : number + 1, :], (LANES, LANES))
            held[number * LANES : (number + 1) * LANES, :] = jnp.transpose(line)
        out[...] = held[own, :]


def first_call(matrix, gain, cubic, share):
    rows = matrix.shape[1]
    lines = (rows // LANES, LANES)
    return pl.pallas_call(
        first_kernel,
        out_shape=[jax.ShapeDtypeStruct((8, LANES), jnp.float32)]
        + [jax.ShapeDtypeStruct((share, LANES), jnp.float32)] * 2,
        in_specs=[IN_VMEM] * 3,
        out_specs=[IN_VMEM] * 3,
        scratch_shapes=[pltpu.VMEM((rows, LANES), jnp.float32)],
        compiler_params=pltpu.CompilerParams(vmem_limit_bytes=VMEM_BYTES),
        cost_estimate=SHORT,
    )(matrix, gain.reshape(lines), cubic.reshape(lines))


def past_kernel(number, opening, steps, layers, fanout, delays, tile, matrix, front, back, mark, *refs):
    refs = list(refs)
    carried = None if opening else refs.pop(0)
    incident = refs.pop(0) if len(steps) == 1 else None
    slots = matrix.shape[0]
    depth, half, waves = front.shape
    layer, lane, col = whereabouts(fanout)
    count = matrix.shape[2] // (2 * half)
    here = cycle_place(layers, layer, lane)
    left, right = [], []
    for side, piece in enumerate((front, back)):
        if count == 1:
            place = side
        else:
            walked = lax.rem(here + (number if side else count - number), count)
            place = 2 * cycle_row(layers, fanout, walked) + side
        columns = pl.ds(pl.multiple_of(place * half, half), half)
        for slot in range(slots):
            delay = delays[slot]
            parts = []
            if 0 in steps:
                parts.append(piece[depth - delay])
            if 1 in steps:
                later = piece[jnp.minimum(depth + 1 - delay, depth - 1)]
                parts.append(jnp.where(delay >= 2, later, jnp.zeros_like(later)))
            right.append(jnp.concatenate(parts, axis=1))
            left.append(matrix[slot, :, columns])
    left, right = jnp.concatenate(left, axis=1), jnp.concatenate(right, axis=0)
    total = jnp.dot(left, right, preferred_element_type=jnp.float32)
    if len(steps) == 2:
        refs[0][...] = total if opening else total + carried[...]
        refs[1][...] = jnp.zeros_like(refs[1])
        return
    if not opening:
        total = total + carried[:, steps[0] * waves : (steps[0] + 1) * waves]
    total = -tile[0].astype(jnp.float32) * total
    share = incident.shape[1]
    if steps[0]:
        refs[0][...] = total
        refs[0][pl.ds(pl.multiple_of(col * share, share), share), :] += incident[1]
        return
    kept, sent, held = refs
    held[...] = total
    bit = lax.rem(col, 2)
    for pair in range(kept.shape[0]):
        for out, which in ((kept, bit), (sent, 1 - bit)):
            rows = pl.ds(pl.multiple_of((2 * pair + which) * share, share), share)
            out[pair] = held[rows, :]
    kept[lax.div(col, 2)] += incident[0]


def past_call(delays, tile, matrix, pieces, mark, carried, incident, number, steps, layers, fanout):
    slots, rows, _ = matrix.shape
    _, half, waves = pieces[0].shape
    totals = jax.ShapeDtypeStruct((rows, 2 * waves), jnp.float32)
    operands = [delays, tile, matrix, *pieces, mark]
    aliases, scratch = {}, []
    if carried is not None:
        operands.append(carried)
    if len(steps) == 2:
        ends = [totals, jax.ShapeDtypeStruct((8, LANES), jnp.float32)]
        aliases = {} if carried is None else {6: 0}
    else:
        operands.append(incident)
        share = incident.shape[1]
        if steps[0]:
            ends = [jax.ShapeDtypeStruct((rows, waves), jnp.float32)]
        else:
            ends = [jax.ShapeDtypeStruct((rows // share // 2, share, waves), jnp.float32)] * 2
            scratch = [pltpu.VMEM((rows, waves), jnp.float32)]
    return pl.pallas_call(
        functools.partial(past_kernel, number, carried is None, steps, layers, fanout),
        out_shape=ends,
        in_specs=[IN_SMEM] * 2 + [IN_VMEM] * (len(operands) - 2),
        out_specs=[IN_VMEM] * len(ends),
        scratch_shapes=scratch,
        input_output_aliases=aliases,
        compiler_params=pltpu.CompilerParams(vmem_limit_bytes=VMEM_BYTES),
        cost_estimate=pl.CostEstimate(
            flops=4 * slots * rows * half * waves * len(steps),
            bytes_accessed=4 * slots * rows * half,
            transcendentals=0,
        ),
    )(*operands)


def small_call(kernel, shapes, matrix, *operands):
    return pl.pallas_call(
        kernel,
        out_shape=shapes,
        in_specs=[IN_VMEM] * (1 + len(operands)),
        out_specs=[IN_VMEM] * len(shapes),
        compiler_params=pltpu.CompilerParams(vmem_limit_bytes=VMEM_BYTES),
        cost_estimate=SHORT,
    )(matrix, *operands)


def fold_kernel(bit, last, matrix, kept, got, kept_out, sent_out):
    own = lax.rem(lax.div(lax.axis_index("col"), bit), 2)
    for pair in range(kept_out.shape[0]):
        kept_out[pair] = kept[2 * pair + own] + got[2 * pair + own]
        sent = kept[2 * pair + 1 - own] + got[2 * pair + 1 - own]
        if not last:
            sent_out[pair] = sent
            continue
        rows = sent.shape[0]
        peak = jnp.maximum(jnp.max(jnp.abs(sent), axis=0, keepdims=True), 1e-30)
        power = jnp.ceil(jnp.log2(peak))
        coded = jnp.round(sent * (jnp.exp2(-power) * LEVELS))
        sent_out[:rows] = coded.astype(jnp.int32).astype(jnp.int16)
        sent_out[rows:] = jnp.broadcast_to(power, (TILE, sent.shape[1])).astype(jnp.int32).astype(jnp.int16)


def fold_call(matrix, kept, got, bit, last):
    pairs, (share, waves) = kept.shape[0] // 2, kept.shape[1:]
    shapes = [jax.ShapeDtypeStruct((pairs, share, waves), jnp.float32)]
    if last:
        shapes.append(jax.ShapeDtypeStruct((share + TILE, waves), jnp.int16))
    else:
        shapes.append(shapes[0])
    return small_call(functools.partial(fold_kernel, bit, last), shapes, matrix, kept, got)


def load_kernel(matrix, kept, got, gain, cubic, out):
    share, waves = out.shape
    gain, cubic = (jnp.concatenate([ref[...]] * (waves // LANES), axis=1) for ref in (gain, cubic))
    power = got[share:].astype(jnp.int32).astype(jnp.float32)[:1]
    field = kept[0] + got[:share].astype(jnp.int32).astype(jnp.float32) * (jnp.exp2(power) * (1.0 / LEVELS))
    out[...] = (gain * field - cubic * field * field * field).astype(jnp.bfloat16)


def load_call(matrix, kept, got, gain, cubic):
    shapes = [jax.ShapeDtypeStruct(kept.shape[1:], jnp.bfloat16)]
    return small_call(load_kernel, shapes, matrix, kept, got, gain, cubic)[0]


def arrange_kernel(layers, fanout, matrix, *refs):
    layer, _, col = whereabouts(fanout)
    apart = layer ^ col
    for place in range(layers):
        @pl.when(apart == place)
        def _():
            for other in range(layers):
                refs[layers + other][...] = refs[place ^ other][...]


def arrange_call(matrix, values, fanout):
    shapes = [jax.ShapeDtypeStruct(value.shape, value.dtype) for value in values]
    return small_call(functools.partial(arrange_kernel, len(values), fanout), shapes, matrix, *values)


def recent_kernel(fanout, beside, ending, pieces, delays, tile, matrix, *refs):
    sources, base, refs = refs[:pieces], refs[pieces], list(refs[pieces + 1 :])
    outs = [refs.pop(0) for _ in range(2 if ending else 1)]
    total, held = refs
    slots = matrix.shape[0]
    _, lane, col = whereabouts(fanout)
    depth, share = held.shape[0], sources[0].shape[0]
    for other, source in enumerate(sources):
        held[pl.ds(pl.multiple_of((col ^ other) * share, share), share), :] = source[...]
    lane = lax.rem(lane + beside, fanout)
    columns = pl.ds(pl.multiple_of(lane * depth, depth), depth)
    total[...] = jnp.zeros_like(total)
    for slot in range(slots):
        @pl.when(delays[slot] == 1)
        def _():
            total[...] += jnp.dot(matrix[slot, :, columns], held[...], preferred_element_type=jnp.float32)

    weight = -tile[0].astype(jnp.float32)
    if not ending:
        outs[0][...] = base[...] + weight * total[...]
        return
    bit = lax.rem(col, 2)
    for pair in range(outs[0].shape[0]):
        for out, own in ((outs[0], bit), (outs[1], 1 - bit)):
            rows = pl.ds(pl.multiple_of((2 * pair + own) * share, share), share)
            out[pair] = base[rows, :] + weight * total[rows, :]


def recent_call(delays, tile, matrix, sources, base, beside, fanout, cols_count):
    slots, rows, depth = matrix.shape
    waves = base.shape[1]
    depth = depth // fanout
    ending = beside == fanout - 1
    if ending:
        ends = [jax.ShapeDtypeStruct((cols_count // 2, rows // cols_count, waves), jnp.float32)] * 2
    else:
        ends = [jax.ShapeDtypeStruct(base.shape, jnp.float32)]
    return pl.pallas_call(
        functools.partial(recent_kernel, fanout, beside, ending, len(sources)),
        out_shape=ends,
        in_specs=[IN_SMEM] * 2 + [IN_VMEM] * (len(sources) + 2),
        out_specs=[IN_VMEM] * len(ends),
        scratch_shapes=[pltpu.VMEM((rows, waves), jnp.float32), pltpu.VMEM((depth, waves), jnp.bfloat16)],
        compiler_params=pltpu.CompilerParams(vmem_limit_bytes=VMEM_BYTES),
        cost_estimate=SHORT,
    )(delays, tile, matrix, *sources, base)


def per_device(rows_count, cols_count, interaction, history, incident, load_gain, load_cubic, delays, tile_map):
    fanout = rows_count // cols_count
    layers = cols_count
    share = incident.shape[1]
    delay, tile = delays.reshape(-1), tile_map.reshape(-1)
    bits = [1 << bit for bit in range((cols_count - 1).bit_length())]

    def send(value, target):
        pairs = []
        for row in range(rows_count):
            for col in range(cols_count):
                goal = target(row // fanout, row % fanout, col)
                if goal is not None:
                    pairs.append((row * cols_count + col, (goal[0] * fanout + goal[1]) * cols_count + goal[2]))
        return lax.ppermute(value, BOTH, pairs)

    cycle = [
        (layer if lane % 2 == 0 else layers - 1 - layer) * fanout + lane
        for lane in range(fanout)
        for layer in range(layers)
    ]
    spot = {row: place for place, row in enumerate(cycle)}

    def around(value, steps):
        pairs = [(row, cycle[(spot[row] + steps) % rows_count]) for row in range(rows_count)]
        return lax.ppermute(value, "row", pairs)

    aligned = history.shape[1] % 256 == 0

    def in_row_order(values, sense):
        row = lax.axis_index("row")
        here = jnp.asarray([spot[row] for row in range(rows_count)], jnp.int32)[row]
        rows = jnp.asarray(cycle, jnp.int32)[(here - sense * jnp.arange(rows_count)) % rows_count]
        return jnp.take(jnp.stack(values), jnp.argsort(rows), axis=0)

    mark, gain, cubic = first_call(interaction, load_gain, load_cubic, share)

    def folded(kept, sent):
        for bit in bits[:-1]:
            got = send(sent, lambda layer, lane, col: (layer, lane, col ^ bit))
            kept, sent = fold_call(interaction, kept, got, 2 * bit, 2 * bit == bits[-1])
        return kept, sent

    def last_hop(sent):
        return send(sent, lambda layer, lane, col: (layer, lane, col ^ bits[-1]))

    def to_layers(current):
        by_layer = {0: current}
        for bit in reversed(bits):
            for apart in list(by_layer):
                value = by_layer[apart]
                if apart and bit in by_layer:
                    value, by_layer[bit] = lax.optimization_barrier((value, by_layer[bit]))
                by_layer[apart ^ bit] = send(value, lambda layer, lane, col: (layer ^ bit, lane, col))
        return by_layer

    def to_sources(ordered):
        lanes = [None] * fanout
        for beside in reversed(range(fanout)):
            lanes[beside] = [
                send(ordered[other], lambda layer, lane, col: (layer, (lane - beside) % fanout, col ^ other))
                if beside or other
                else ordered[0]
                for other in range(cols_count)
            ]
        return lanes

    chunks = split_waves(history.shape[2])
    half = history.shape[1] // 2
    moving = [(history[:, :half, start:stop], history[:, half:, start:stop]) for start, stop in chunks]
    carried, marks = [None] * len(chunks), [None] * len(chunks)
    arrived = [[moving[number]] for number in range(len(chunks))]

    def add_piece(number, step):
        start, stop = chunks[number]
        outs = past_call(
            delay,
            tile,
            interaction,
            arrived[number][step],
            marks[number],
            carried[number],
            None,
            step,
            (0, 1),
            layers,
            fanout,
        )
        carried[number], marks[number] = outs

    marks = [mark] * len(chunks)
    added = [0] * len(chunks)
    for step in range(1, rows_count):
        for number in range(len(chunks)):
            front, back = arrived[number][-1]
            if step >= 2 and aligned:
                wanted = 0 if step == 2 else 1 if step == 3 else step - 1
                while added[number] < wanted:
                    add_piece(number, added[number])
                    added[number] += 1
                front, back, marks[number] = lax.optimization_barrier((front, back, marks[number]))
            arrived[number].append((around(front, 1), around(back, -1)))
    last = rows_count - 1
    for number, (start, stop) in enumerate(chunks):
        if aligned:
            for step in range(added[number], last):
                add_piece(number, step)
            arrived[number] = arrived[number][last]
        else:
            fronts, backs = zip(*arrived[number])
            ordered = jnp.stack([in_row_order(fronts, 1), in_row_order(backs, -1)], axis=1)
            ordered = jnp.moveaxis(ordered, 2, 0).reshape(history.shape[0], 2, rows_count * half, stop - start)
            arrived[number] = ordered[:, 0], ordered[:, 1]

    def end_past(number, step):
        start, stop = chunks[number]
        return past_call(
            delay,
            tile,
            interaction,
            arrived[number],
            marks[number],
            carried[number],
            incident[:, :, start:stop],
            last,
            (step,),
            layers,
            fanout,
        )

    numbers = range(len(chunks))
    kepts, sents = [None] * len(chunks), [None] * len(chunks)
    for number in numbers:
        kepts[number], sents[number] = folded(*end_past(number, 0))
    gots, laters = [], []
    for number in numbers:
        gots.append(last_hop(sents[number]))
        sents[number], marks[number] = lax.optimization_barrier((sents[number], marks[number]))
        laters.append(end_past(number, 1)[0])
    by_layers = [to_layers(load_call(interaction, kepts[number], gots[number], gain, cubic)) for number in numbers]
    every, ends = [], []
    for number in numbers:
        ordered = arrange_call(interaction, [by_layers[number][apart] for apart in range(layers)], fanout)
        if number:
            ordered, ends[-1] = lax.optimization_barrier((ordered, ends[-1]))
        every.append(to_sources(ordered))
        ends.append(
            recent_call(delay, tile, interaction, every[number][0], laters[number], 0, fanout, cols_count)
        )
    for number in numbers:
        for beside in range(1, fanout):
            ends[number] = recent_call(
                delay, tile, interaction, every[number][beside], ends[number][0], beside, fanout, cols_count
            )
        kepts[number], sents[number] = folded(*ends[number])
    gots = [last_hop(sents[number]) for number in numbers]
    lasts = [load_call(interaction, kepts[number], gots[number], gain, cubic) for number in numbers]
    results = [jnp.stack([by_layer[0], last]) for by_layer, last in zip(by_layers, lasts)]
    return jnp.concatenate(results, axis=2)


def solution(mesh):
    placed = (
        P(None, "row", "col"),
        P(None, ("col", "row"), None),
        P(None, ("row", "col"), None),
        P("row"),
        P("row"),
        P("row", "col", None),
        P("row", "col"),
    )
    return jax.shard_map(
        functools.partial(per_device, mesh.shape["row"], mesh.shape["col"]),
        mesh=mesh,
        in_specs=placed,
        out_specs=P(None, ("row", "col"), None),
        check_vma=False,
    )
```

```python
import functools

import jax
import jax.numpy as jnp
from jax import lax
from jax.experimental import pallas as pl
from jax.experimental.pallas import tpu as pltpu
from jax.sharding import PartitionSpec as P

BOTH = ("row", "col")
VMEM_BYTES = 8 * 1024 * 1024
TILE = 16
ROWS = 256
SHORT = pl.CostEstimate(flops=0, bytes_accessed=0, transcendentals=0)
LANES = 128
LEVELS = 32000.0
IN_VMEM = pl.BlockSpec(memory_space=pltpu.VMEM)
IN_SMEM = pl.BlockSpec(memory_space=pltpu.SMEM)


def split_waves(waves):
    unit = 128
    if waves % unit or waves < 2 * unit:
        return [(0, waves)]
    half = (waves // unit + 1) // 2 * unit
    return [(0, half), (half, waves)]


def whereabouts(fanout):
    row = lax.axis_index("row")
    return lax.div(row, fanout), lax.rem(row, fanout), lax.axis_index("col")


def cycle_row(layers, fanout, place):
    lane, along = lax.div(place, layers), lax.rem(place, layers)
    return jnp.where(lax.rem(lane, 2) == 0, along, layers - 1 - along) * fanout + lane


def cycle_place(layers, layer, lane):
    return lane * layers + jnp.where(lax.rem(lane, 2) == 0, layer, layers - 1 - layer)


def first_kernel(matrix, gain, cubic, mark, own_gain, own_cubic, held):
    mark[...] = matrix[0, :8, :128].astype(jnp.float32)
    share = own_gain.shape[0]
    own = pl.ds(pl.multiple_of(lax.axis_index("col") * share, share), share)
    for source, out in ((gain, own_gain), (cubic, own_cubic)):
        for number in range(source.shape[0]):
            line = jnp.broadcast_to(source[number : number + 1, :], (LANES, LANES))
            held[number * LANES : (number + 1) * LANES, :] = jnp.transpose(line)
        out[...] = held[own, :]


def first_call(matrix, gain, cubic, share):
    rows = matrix.shape[1]
    lines = (rows // LANES, LANES)
    return pl.pallas_call(
        first_kernel,
        out_shape=[jax.ShapeDtypeStruct((8, LANES), jnp.float32)]
        + [jax.ShapeDtypeStruct((share, LANES), jnp.float32)] * 2,
        in_specs=[IN_VMEM] * 3,
        out_specs=[IN_VMEM] * 3,
        scratch_shapes=[pltpu.VMEM((rows, LANES), jnp.float32)],
        compiler_params=pltpu.CompilerParams(vmem_limit_bytes=VMEM_BYTES),
        cost_estimate=SHORT,
    )(matrix, gain.reshape(lines), cubic.reshape(lines))


def past_kernel(number, opening, steps, layers, fanout, delays, tile, matrix, front, back, mark, *refs):
    refs = list(refs)
    carried = None if opening else refs.pop(0)
    incident = refs.pop(0) if len(steps) == 1 else None
    slots = matrix.shape[0]
    depth, half, waves = front.shape
    layer, lane, col = whereabouts(fanout)
    count = matrix.shape[2] // (2 * half)
    here = cycle_place(layers, layer, lane)
    right, columns = [], []
    for side, piece in enumerate((front, back)):
        if count == 1:
            place = side
        else:
            walked = lax.rem(here + (number if side else count - number), count)
            place = 2 * cycle_row(layers, fanout, walked) + side
        columns.append(pl.ds(pl.multiple_of(place * half, half), half))
        for slot in range(slots):
            delay = delays[slot]
            parts = []
            if 0 in steps:
                parts.append(piece[depth - delay])
            if 1 in steps:
                later = piece[jnp.minimum(depth + 1 - delay, depth - 1)]
                parts.append(jnp.where(delay >= 2, later, jnp.zeros_like(later)))
            right.append(jnp.concatenate(parts, axis=1))
    right = jnp.concatenate(right, axis=0)
    span = slice(None) if len(steps) == 2 else slice(steps[0] * waves, (steps[0] + 1) * waves)
    total = refs[-1] if steps == (0,) else refs[0]
    weight = 1.0 if len(steps) == 2 else -tile[0].astype(jnp.float32)

    def some_rows(turn, _):
        rows = pl.ds(pl.multiple_of(turn * ROWS, ROWS), ROWS)
        left = jnp.concatenate([matrix[slot, rows, line] for line in columns for slot in range(slots)], axis=1)
        added = jnp.dot(left, right, preferred_element_type=jnp.float32)
        if not opening:
            added = added + carried[rows, span]
        total[rows, :] = added if len(steps) == 2 else weight * added
        return 0

    lax.fori_loop(0, matrix.shape[1] // ROWS, some_rows, 0)
    if len(steps) == 2:
        refs[1][...] = jnp.zeros_like(refs[1])
        return
    share = incident.shape[1]
    if steps[0]:
        total[pl.ds(pl.multiple_of(col * share, share), share), :] += incident[1]
        return
    kept, sent, held = refs
    bit = lax.rem(col, 2)
    for pair in range(kept.shape[0]):
        for out, which in ((kept, bit), (sent, 1 - bit)):
            rows = pl.ds(pl.multiple_of((2 * pair + which) * share, share), share)
            out[pair] = held[rows, :]
    kept[lax.div(col, 2)] += incident[0]


def past_call(delays, tile, matrix, pieces, mark, carried, incident, number, steps, layers, fanout):
    slots, rows, _ = matrix.shape
    _, half, waves = pieces[0].shape
    totals = jax.ShapeDtypeStruct((rows, 2 * waves), jnp.float32)
    operands = [delays, tile, matrix, *pieces, mark]
    aliases, scratch = {}, []
    if carried is not None:
        operands.append(carried)
    if len(steps) == 2:
        ends = [totals, jax.ShapeDtypeStruct((8, LANES), jnp.float32)]
        aliases = {} if carried is None else {6: 0}
    else:
        operands.append(incident)
        share = incident.shape[1]
        if steps[0]:
            ends = [jax.ShapeDtypeStruct((rows, waves), jnp.float32)]
        else:
            ends = [jax.ShapeDtypeStruct((rows // share // 2, share, waves), jnp.float32)] * 2
            scratch = [pltpu.VMEM((rows, waves), jnp.float32)]
    return pl.pallas_call(
        functools.partial(past_kernel, number, carried is None, steps, layers, fanout),
        out_shape=ends,
        in_specs=[IN_SMEM] * 2 + [IN_VMEM] * (len(operands) - 2),
        out_specs=[IN_VMEM] * len(ends),
        scratch_shapes=scratch,
        input_output_aliases=aliases,
        compiler_params=pltpu.CompilerParams(vmem_limit_bytes=VMEM_BYTES),
        cost_estimate=pl.CostEstimate(
            flops=4 * slots * rows * half * waves * len(steps),
            bytes_accessed=4 * slots * rows * half,
            transcendentals=0,
        ),
    )(*operands)


def small_call(kernel, shapes, matrix, *operands):
    return pl.pallas_call(
        kernel,
        out_shape=shapes,
        in_specs=[IN_VMEM] * (1 + len(operands)),
        out_specs=[IN_VMEM] * len(shapes),
        compiler_params=pltpu.CompilerParams(vmem_limit_bytes=VMEM_BYTES),
        cost_estimate=SHORT,
    )(matrix, *operands)


def fold_kernel(bit, last, matrix, kept, got, kept_out, sent_out):
    own = lax.rem(lax.div(lax.axis_index("col"), bit), 2)
    for pair in range(kept_out.shape[0]):
        kept_out[pair] = kept[2 * pair + own] + got[2 * pair + own]
        sent = kept[2 * pair + 1 - own] + got[2 * pair + 1 - own]
        if not last:
            sent_out[pair] = sent
            continue
        rows = sent.shape[0]
        peak = jnp.maximum(jnp.max(jnp.abs(sent), axis=0, keepdims=True), 1e-30)
        power = jnp.ceil(jnp.log2(peak))
        coded = jnp.round(sent * (jnp.exp2(-power) * LEVELS))
        sent_out[:rows] = coded.astype(jnp.int32).astype(jnp.int16)
        sent_out[rows:] = jnp.broadcast_to(power, (TILE, sent.shape[1])).astype(jnp.int32).astype(jnp.int16)


def fold_call(matrix, kept, got, bit, last):
    pairs, (share, waves) = kept.shape[0] // 2, kept.shape[1:]
    shapes = [jax.ShapeDtypeStruct((pairs, share, waves), jnp.float32)]
    if last:
        shapes.append(jax.ShapeDtypeStruct((share + TILE, waves), jnp.int16))
    else:
        shapes.append(shapes[0])
    return small_call(functools.partial(fold_kernel, bit, last), shapes, matrix, kept, got)


def load_kernel(matrix, kept, got, gain, cubic, out):
    share, waves = out.shape
    gain, cubic = (jnp.concatenate([ref[...]] * (waves // LANES), axis=1) for ref in (gain, cubic))
    power = got[share:].astype(jnp.int32).astype(jnp.float32)[:1]
    field = kept[0] + got[:share].astype(jnp.int32).astype(jnp.float32) * (jnp.exp2(power) * (1.0 / LEVELS))
    out[...] = (gain * field - cubic * field * field * field).astype(jnp.bfloat16)


def load_call(matrix, kept, got, gain, cubic):
    shapes = [jax.ShapeDtypeStruct(kept.shape[1:], jnp.bfloat16)]
    return small_call(load_kernel, shapes, matrix, kept, got, gain, cubic)[0]


def arrange_kernel(layers, fanout, matrix, *refs):
    layer, _, col = whereabouts(fanout)
    apart = layer ^ col
    for place in range(layers):
        @pl.when(apart == place)
        def _():
            for other in range(layers):
                refs[layers + other][...] = refs[place ^ other][...]


def arrange_call(matrix, values, fanout):
    shapes = [jax.ShapeDtypeStruct(value.shape, value.dtype) for value in values]
    return small_call(functools.partial(arrange_kernel, len(values), fanout), shapes, matrix, *values)


def recent_kernel(fanout, beside, ending, pieces, delays, tile, matrix, *refs):
    sources, base, refs = refs[:pieces], refs[pieces], list(refs[pieces + 1 :])
    outs = [refs.pop(0) for _ in range(2 if ending else 1)]
    total, held = refs
    slots = matrix.shape[0]
    _, lane, col = whereabouts(fanout)
    depth, share = held.shape[0], sources[0].shape[0]
    for other, source in enumerate(sources):
        held[pl.ds(pl.multiple_of((col ^ other) * share, share), share), :] = source[...]
    lane = lax.rem(lane + beside, fanout)
    columns = pl.ds(pl.multiple_of(lane * depth, depth), depth)
    total[...] = jnp.zeros_like(total)

    def some_slot(slot, _):
        @pl.when(delays[slot] == 1)
        def _():
            total[...] += jnp.dot(matrix[slot, :, columns], held[...], preferred_element_type=jnp.float32)

        return 0

    lax.fori_loop(0, slots, some_slot, 0)
    weight = -tile[0].astype(jnp.float32)
    if not ending:
        outs[0][...] = base[...] + weight * total[...]
        return
    bit = lax.rem(col, 2)
    for pair in range(outs[0].shape[0]):
        for out, own in ((outs[0], bit), (outs[1], 1 - bit)):
            rows = pl.ds(pl.multiple_of((2 * pair + own) * share, share), share)
            out[pair] = base[rows, :] + weight * total[rows, :]


def recent_call(delays, tile, matrix, sources, base, beside, fanout, cols_count):
    slots, rows, depth = matrix.shape
    waves = base.shape[1]
    depth = depth // fanout
    ending = beside == fanout - 1
    if ending:
        ends = [jax.ShapeDtypeStruct((cols_count // 2, rows // cols_count, waves), jnp.float32)] * 2
    else:
        ends = [jax.ShapeDtypeStruct(base.shape, jnp.float32)]
    return pl.pallas_call(
        functools.partial(recent_kernel, fanout, beside, ending, len(sources)),
        out_shape=ends,
        in_specs=[IN_SMEM] * 2 + [IN_VMEM] * (len(sources) + 2),
        out_specs=[IN_VMEM] * len(ends),
        scratch_shapes=[pltpu.VMEM((rows, waves), jnp.float32), pltpu.VMEM((depth, waves), jnp.bfloat16)],
        compiler_params=pltpu.CompilerParams(vmem_limit_bytes=VMEM_BYTES),
        cost_estimate=SHORT,
    )(delays, tile, matrix, *sources, base)


def per_device(rows_count, cols_count, interaction, history, incident, load_gain, load_cubic, delays, tile_map):
    fanout = rows_count // cols_count
    layers = cols_count
    share = incident.shape[1]
    delay, tile = delays.reshape(-1), tile_map.reshape(-1)
    bits = [1 << bit for bit in range((cols_count - 1).bit_length())]

    def send(value, target):
        pairs = []
        for row in range(rows_count):
            for col in range(cols_count):
                goal = target(row // fanout, row % fanout, col)
                if goal is not None:
                    pairs.append((row * cols_count + col, (goal[0] * fanout + goal[1]) * cols_count + goal[2]))
        return lax.ppermute(value, BOTH, pairs)

    cycle = [
        (layer if lane % 2 == 0 else layers - 1 - layer) * fanout + lane
        for lane in range(fanout)
        for layer in range(layers)
    ]
    spot = {row: place for place, row in enumerate(cycle)}

    def around(value, steps):
        pairs = [(row, cycle[(spot[row] + steps) % rows_count]) for row in range(rows_count)]
        return lax.ppermute(value, "row", pairs)

    aligned = history.shape[1] % 256 == 0

    def in_row_order(values, sense):
        row = lax.axis_index("row")
        here = jnp.asarray([spot[row] for row in range(rows_count)], jnp.int32)[row]
        rows = jnp.asarray(cycle, jnp.int32)[(here - sense * jnp.arange(rows_count)) % rows_count]
        return jnp.take(jnp.stack(values), jnp.argsort(rows), axis=0)

    mark, gain, cubic = first_call(interaction, load_gain, load_cubic, share)

    def folded(kept, sent):
        for bit in bits[:-1]:
            got = send(sent, lambda layer, lane, col: (layer, lane, col ^ bit))
            kept, sent = fold_call(interaction, kept, got, 2 * bit, 2 * bit == bits[-1])
        return kept, sent

    def last_hop(sent):
        return send(sent, lambda layer, lane, col: (layer, lane, col ^ bits[-1]))

    def to_layers(current):
        by_layer = {0: current}
        for bit in reversed(bits):
            for apart in list(by_layer):
                value = by_layer[apart]
                if apart and bit in by_layer:
                    value, by_layer[bit] = lax.optimization_barrier((value, by_layer[bit]))
                by_layer[apart ^ bit] = send(value, lambda layer, lane, col: (layer ^ bit, lane, col))
        return by_layer

    def to_sources(ordered):
        lanes = [None] * fanout
        for beside in reversed(range(fanout)):
            lanes[beside] = [
                send(ordered[other], lambda layer, lane, col: (layer, (lane - beside) % fanout, col ^ other))
                if beside or other
                else ordered[0]
                for other in range(cols_count)
            ]
        return lanes

    chunks = split_waves(history.shape[2])
    half = history.shape[1] // 2
    moving = [(history[:, :half, start:stop], history[:, half:, start:stop]) for start, stop in chunks]
    carried, marks = [None] * len(chunks), [None] * len(chunks)
    arrived = [[moving[number]] for number in range(len(chunks))]

    def add_piece(number, step):
        start, stop = chunks[number]
        outs = past_call(
            delay,
            tile,
            interaction,
            arrived[number][step],
            marks[number],
            carried[number],
            None,
            step,
            (0, 1),
            layers,
            fanout,
        )
        carried[number], marks[number] = outs

    marks = [mark] * len(chunks)
    added = [0] * len(chunks)
    for step in range(1, rows_count):
        for number in range(len(chunks)):
            front, back = arrived[number][-1]
            if step >= 2 and aligned:
                wanted = 0 if step == 2 else 1 if step == 3 else step - 1
                while added[number] < wanted:
                    add_piece(number, added[number])
                    added[number] += 1
                front, back, marks[number] = lax.optimization_barrier((front, back, marks[number]))
            arrived[number].append((around(front, 1), around(back, -1)))
    last = rows_count - 1
    for number, (start, stop) in enumerate(chunks):
        if aligned:
            for step in range(added[number], last):
                add_piece(number, step)
            arrived[number] = arrived[number][last]
        else:
            fronts, backs = zip(*arrived[number])
            ordered = jnp.stack([in_row_order(fronts, 1), in_row_order(backs, -1)], axis=1)
            ordered = jnp.moveaxis(ordered, 2, 0).reshape(history.shape[0], 2, rows_count * half, stop - start)
            arrived[number] = ordered[:, 0], ordered[:, 1]

    def end_past(number, step):
        start, stop = chunks[number]
        return past_call(
            delay,
            tile,
            interaction,
            arrived[number],
            marks[number],
            carried[number],
            incident[:, :, start:stop],
            last,
            (step,),
            layers,
            fanout,
        )

    numbers = range(len(chunks))
    kepts, sents = [None] * len(chunks), [None] * len(chunks)
    for number in numbers:
        kepts[number], sents[number] = folded(*end_past(number, 0))
    gots, laters = [], []
    for number in numbers:
        gots.append(last_hop(sents[number]))
        sents[number], marks[number] = lax.optimization_barrier((sents[number], marks[number]))
        laters.append(end_past(number, 1)[0])
    by_layers = [to_layers(load_call(interaction, kepts[number], gots[number], gain, cubic)) for number in numbers]
    every, ends = [], []
    for number in numbers:
        ordered = arrange_call(interaction, [by_layers[number][apart] for apart in range(layers)], fanout)
        if number:
            ordered, ends[-1] = lax.optimization_barrier((ordered, ends[-1]))
        every.append(to_sources(ordered))
        ends.append(
            recent_call(delay, tile, interaction, every[number][0], laters[number], 0, fanout, cols_count)
        )
    for number in numbers:
        for beside in range(1, fanout):
            ends[number] = recent_call(
                delay, tile, interaction, every[number][beside], ends[number][0], beside, fanout, cols_count
            )
        kepts[number], sents[number] = folded(*ends[number])
    gots = [last_hop(sents[number]) for number in numbers]
    lasts = [load_call(interaction, kepts[number], gots[number], gain, cubic) for number in numbers]
    results = [jnp.stack([by_layer[0], last]) for by_layer, last in zip(by_layers, lasts)]
    return jnp.concatenate(results, axis=2)


def solution(mesh):
    placed = (
        P(None, "row", "col"),
        P(None, ("col", "row"), None),
        P(None, ("row", "col"), None),
        P("row"),
        P("row"),
        P("row", "col", None),
        P("row", "col"),
    )
    return jax.shard_map(
        functools.partial(per_device, mesh.shape["row"], mesh.shape["col"]),
        mesh=mesh,
        in_specs=placed,
        out_specs=P(None, ("row", "col"), None),
        check_vma=False,
    )
```

```python
import functools

import jax
import jax.numpy as jnp
from jax import lax
from jax.experimental import pallas as pl
from jax.experimental.pallas import tpu as pltpu
from jax.sharding import PartitionSpec as P

BOTH = ("row", "col")
VMEM_BYTES = 8 * 1024 * 1024
TILE = 16
ROWS = 512
SHORT = pl.CostEstimate(flops=0, bytes_accessed=0, transcendentals=0)
LANES = 128
LEVELS = 32000.0
IN_VMEM = pl.BlockSpec(memory_space=pltpu.VMEM)
IN_SMEM = pl.BlockSpec(memory_space=pltpu.SMEM)


def split_waves(waves):
    unit = 128
    if waves % unit or waves < 2 * unit:
        return [(0, waves)]
    half = (waves // unit + 1) // 2 * unit
    return [(0, half), (half, waves)]


def whereabouts(fanout):
    row = lax.axis_index("row")
    return lax.div(row, fanout), lax.rem(row, fanout), lax.axis_index("col")


def cycle_row(layers, fanout, place):
    lane, along = lax.div(place, layers), lax.rem(place, layers)
    return jnp.where(lax.rem(lane, 2) == 0, along, layers - 1 - along) * fanout + lane


def cycle_place(layers, layer, lane):
    return lane * layers + jnp.where(lax.rem(lane, 2) == 0, layer, layers - 1 - layer)


def first_kernel(matrix, gain, cubic, mark, own_gain, own_cubic, held):
    mark[...] = matrix[0, :8, :128].astype(jnp.float32)
    share = own_gain.shape[0]
    own = pl.ds(pl.multiple_of(lax.axis_index("col") * share, share), share)
    for source, out in ((gain, own_gain), (cubic, own_cubic)):
        for number in range(source.shape[0]):
            line = jnp.broadcast_to(source[number : number + 1, :], (LANES, LANES))
            held[number * LANES : (number + 1) * LANES, :] = jnp.transpose(line)
        out[...] = held[own, :]


def first_call(matrix, gain, cubic, share):
    rows = matrix.shape[1]
    lines = (rows // LANES, LANES)
    return pl.pallas_call(
        first_kernel,
        out_shape=[jax.ShapeDtypeStruct((8, LANES), jnp.float32)]
        + [jax.ShapeDtypeStruct((share, LANES), jnp.float32)] * 2,
        in_specs=[IN_VMEM] * 3,
        out_specs=[IN_VMEM] * 3,
        scratch_shapes=[pltpu.VMEM((rows, LANES), jnp.float32)],
        compiler_params=pltpu.CompilerParams(vmem_limit_bytes=VMEM_BYTES),
        cost_estimate=SHORT,
    )(matrix, gain.reshape(lines), cubic.reshape(lines))


def past_kernel(number, opening, steps, layers, fanout, delays, tile, matrix, front, back, mark, *refs):
    refs = list(refs)
    carried = None if opening else refs.pop(0)
    incident = refs.pop(0) if len(steps) == 1 else None
    slots = matrix.shape[0]
    depth, half, waves = front.shape
    layer, lane, col = whereabouts(fanout)
    count = matrix.shape[2] // (2 * half)
    here = cycle_place(layers, layer, lane)
    right, columns = [], []
    for side, piece in enumerate((front, back)):
        if count == 1:
            place = side
        else:
            walked = lax.rem(here + (number if side else count - number), count)
            place = 2 * cycle_row(layers, fanout, walked) + side
        columns.append(pl.ds(pl.multiple_of(place * half, half), half))
        for slot in range(slots):
            delay = delays[slot]
            parts = []
            if 0 in steps:
                parts.append(piece[depth - delay])
            if 1 in steps:
                later = piece[jnp.minimum(depth + 1 - delay, depth - 1)]
                parts.append(jnp.where(delay >= 2, later, jnp.zeros_like(later)))
            right.append(jnp.concatenate(parts, axis=1))
    right = jnp.concatenate(right, axis=0)
    span = slice(None) if len(steps) == 2 else slice(steps[0] * waves, (steps[0] + 1) * waves)
    total = refs[-1] if steps == (0,) else refs[0]
    weight = 1.0 if len(steps) == 2 else -tile[0].astype(jnp.float32)

    def some_rows(turn, _):
        rows = pl.ds(pl.multiple_of(turn * ROWS, ROWS), ROWS)
        left = jnp.concatenate([matrix[slot, rows, line] for line in columns for slot in range(slots)], axis=1)
        added = jnp.dot(left, right, preferred_element_type=jnp.float32)
        if not opening:
            added = added + carried[rows, span]
        total[rows, :] = added if len(steps) == 2 else weight * added
        return 0

    lax.fori_loop(0, matrix.shape[1] // ROWS, some_rows, 0)
    if len(steps) == 2:
        refs[1][...] = jnp.zeros_like(refs[1])
        return
    share = incident.shape[1]
    if steps[0]:
        total[pl.ds(pl.multiple_of(col * share, share), share), :] += incident[1]
        return
    kept, sent, held = refs
    bit = lax.rem(col, 2)
    for pair in range(kept.shape[0]):
        for out, which in ((kept, bit), (sent, 1 - bit)):
            rows = pl.ds(pl.multiple_of((2 * pair + which) * share, share), share)
            out[pair] = held[rows, :]
    kept[lax.div(col, 2)] += incident[0]


def past_call(delays, tile, matrix, pieces, mark, carried, incident, number, steps, layers, fanout):
    slots, rows, _ = matrix.shape
    _, half, waves = pieces[0].shape
    totals = jax.ShapeDtypeStruct((rows, 2 * waves), jnp.float32)
    operands = [delays, tile, matrix, *pieces, mark]
    aliases, scratch = {}, []
    if carried is not None:
        operands.append(carried)
    if len(steps) == 2:
        ends = [totals, jax.ShapeDtypeStruct((8, LANES), jnp.float32)]
        aliases = {} if carried is None else {6: 0}
    else:
        operands.append(incident)
        share = incident.shape[1]
        if steps[0]:
            ends = [jax.ShapeDtypeStruct((rows, waves), jnp.float32)]
        else:
            ends = [jax.ShapeDtypeStruct((rows // share // 2, share, waves), jnp.float32)] * 2
            scratch = [pltpu.VMEM((rows, waves), jnp.float32)]
    return pl.pallas_call(
        functools.partial(past_kernel, number, carried is None, steps, layers, fanout),
        out_shape=ends,
        in_specs=[IN_SMEM] * 2 + [IN_VMEM] * (len(operands) - 2),
        out_specs=[IN_VMEM] * len(ends),
        scratch_shapes=scratch,
        input_output_aliases=aliases,
        compiler_params=pltpu.CompilerParams(vmem_limit_bytes=VMEM_BYTES),
        cost_estimate=pl.CostEstimate(
            flops=4 * slots * rows * half * waves * len(steps),
            bytes_accessed=4 * slots * rows * half,
            transcendentals=0,
        ),
    )(*operands)


def small_call(kernel, shapes, matrix, *operands):
    return pl.pallas_call(
        kernel,
        out_shape=shapes,
        in_specs=[IN_VMEM] * (1 + len(operands)),
        out_specs=[IN_VMEM] * len(shapes),
        compiler_params=pltpu.CompilerParams(vmem_limit_bytes=VMEM_BYTES),
        cost_estimate=SHORT,
    )(matrix, *operands)


def fold_kernel(bit, last, matrix, kept, got, kept_out, sent_out):
    own = lax.rem(lax.div(lax.axis_index("col"), bit), 2)
    for pair in range(kept_out.shape[0]):
        kept_out[pair] = kept[2 * pair + own] + got[2 * pair + own]
        sent = kept[2 * pair + 1 - own] + got[2 * pair + 1 - own]
        if not last:
            sent_out[pair] = sent
            continue
        rows = sent.shape[0]
        peak = jnp.maximum(jnp.max(jnp.abs(sent), axis=0, keepdims=True), 1e-30)
        power = jnp.ceil(jnp.log2(peak))
        coded = jnp.round(sent * (jnp.exp2(-power) * LEVELS))
        sent_out[:rows] = coded.astype(jnp.int32).astype(jnp.int16)
        sent_out[rows:] = jnp.broadcast_to(power, (TILE, sent.shape[1])).astype(jnp.int32).astype(jnp.int16)


def fold_call(matrix, kept, got, bit, last):
    pairs, (share, waves) = kept.shape[0] // 2, kept.shape[1:]
    shapes = [jax.ShapeDtypeStruct((pairs, share, waves), jnp.float32)]
    if last:
        shapes.append(jax.ShapeDtypeStruct((share + TILE, waves), jnp.int16))
    else:
        shapes.append(shapes[0])
    return small_call(functools.partial(fold_kernel, bit, last), shapes, matrix, kept, got)


def load_kernel(matrix, kept, got, gain, cubic, out):
    share, waves = out.shape
    gain, cubic = (jnp.concatenate([ref[...]] * (waves // LANES), axis=1) for ref in (gain, cubic))
    power = got[share:].astype(jnp.int32).astype(jnp.float32)[:1]
    field = kept[0] + got[:share].astype(jnp.int32).astype(jnp.float32) * (jnp.exp2(power) * (1.0 / LEVELS))
    out[...] = (gain * field - cubic * field * field * field).astype(jnp.bfloat16)


def load_call(matrix, kept, got, gain, cubic):
    shapes = [jax.ShapeDtypeStruct(kept.shape[1:], jnp.bfloat16)]
    return small_call(load_kernel, shapes, matrix, kept, got, gain, cubic)[0]


def arrange_kernel(layers, fanout, matrix, *refs):
    layer, _, col = whereabouts(fanout)
    apart = layer ^ col
    for place in range(layers):
        @pl.when(apart == place)
        def _():
            for other in range(layers):
                refs[layers + other][...] = refs[place ^ other][...]


def arrange_call(matrix, values, fanout):
    shapes = [jax.ShapeDtypeStruct(value.shape, value.dtype) for value in values]
    return small_call(functools.partial(arrange_kernel, len(values), fanout), shapes, matrix, *values)


def recent_kernel(fanout, beside, ending, pieces, delays, tile, matrix, *refs):
    sources, base, refs = refs[:pieces], refs[pieces], list(refs[pieces + 1 :])
    outs = [refs.pop(0) for _ in range(2 if ending else 1)]
    total, held = refs
    slots = matrix.shape[0]
    _, lane, col = whereabouts(fanout)
    depth, share = held.shape[0], sources[0].shape[0]
    for other, source in enumerate(sources):
        held[pl.ds(pl.multiple_of((col ^ other) * share, share), share), :] = source[...]
    lane = lax.rem(lane + beside, fanout)
    columns = pl.ds(pl.multiple_of(lane * depth, depth), depth)
    total[...] = jnp.zeros_like(total)

    def some_slot(slot, _):
        @pl.when(delays[slot] == 1)
        def _():
            total[...] += jnp.dot(matrix[slot, :, columns], held[...], preferred_element_type=jnp.float32)

        return 0

    lax.fori_loop(0, slots, some_slot, 0)
    weight = -tile[0].astype(jnp.float32)
    if not ending:
        outs[0][...] = base[...] + weight * total[...]
        return
    bit = lax.rem(col, 2)
    for pair in range(outs[0].shape[0]):
        for out, own in ((outs[0], bit), (outs[1], 1 - bit)):
            rows = pl.ds(pl.multiple_of((2 * pair + own) * share, share), share)
            out[pair] = base[rows, :] + weight * total[rows, :]


def recent_call(delays, tile, matrix, sources, base, beside, fanout, cols_count):
    slots, rows, depth = matrix.shape
    waves = base.shape[1]
    depth = depth // fanout
    ending = beside == fanout - 1
    if ending:
        ends = [jax.ShapeDtypeStruct((cols_count // 2, rows // cols_count, waves), jnp.float32)] * 2
    else:
        ends = [jax.ShapeDtypeStruct(base.shape, jnp.float32)]
    return pl.pallas_call(
        functools.partial(recent_kernel, fanout, beside, ending, len(sources)),
        out_shape=ends,
        in_specs=[IN_SMEM] * 2 + [IN_VMEM] * (len(sources) + 2),
        out_specs=[IN_VMEM] * len(ends),
        scratch_shapes=[pltpu.VMEM((rows, waves), jnp.float32), pltpu.VMEM((depth, waves), jnp.bfloat16)],
        compiler_params=pltpu.CompilerParams(vmem_limit_bytes=VMEM_BYTES),
        cost_estimate=SHORT,
    )(delays, tile, matrix, *sources, base)


def per_device(rows_count, cols_count, interaction, history, incident, load_gain, load_cubic, delays, tile_map):
    fanout = rows_count // cols_count
    layers = cols_count
    share = incident.shape[1]
    delay, tile = delays.reshape(-1), tile_map.reshape(-1)
    bits = [1 << bit for bit in range((cols_count - 1).bit_length())]

    def send(value, target):
        pairs = []
        for row in range(rows_count):
            for col in range(cols_count):
                goal = target(row // fanout, row % fanout, col)
                if goal is not None:
                    pairs.append((row * cols_count + col, (goal[0] * fanout + goal[1]) * cols_count + goal[2]))
        return lax.ppermute(value, BOTH, pairs)

    cycle = [
        (layer if lane % 2 == 0 else layers - 1 - layer) * fanout + lane
        for lane in range(fanout)
        for layer in range(layers)
    ]
    spot = {row: place for place, row in enumerate(cycle)}

    def around(value, steps):
        pairs = [(row, cycle[(spot[row] + steps) % rows_count]) for row in range(rows_count)]
        return lax.ppermute(value, "row", pairs)

    aligned = history.shape[1] % 256 == 0

    def in_row_order(values, sense):
        row = lax.axis_index("row")
        here = jnp.asarray([spot[row] for row in range(rows_count)], jnp.int32)[row]
        rows = jnp.asarray(cycle, jnp.int32)[(here - sense * jnp.arange(rows_count)) % rows_count]
        return jnp.take(jnp.stack(values), jnp.argsort(rows), axis=0)

    mark, gain, cubic = first_call(interaction, load_gain, load_cubic, share)

    def folded(kept, sent):
        for bit in bits[:-1]:
            got = send(sent, lambda layer, lane, col: (layer, lane, col ^ bit))
            kept, sent = fold_call(interaction, kept, got, 2 * bit, 2 * bit == bits[-1])
        return kept, sent

    def last_hop(sent):
        return send(sent, lambda layer, lane, col: (layer, lane, col ^ bits[-1]))

    def to_layers(current):
        by_layer = {0: current}
        for bit in reversed(bits):
            for apart in list(by_layer):
                value = by_layer[apart]
                if apart and bit in by_layer:
                    value, by_layer[bit] = lax.optimization_barrier((value, by_layer[bit]))
                by_layer[apart ^ bit] = send(value, lambda layer, lane, col: (layer ^ bit, lane, col))
        return by_layer

    def to_sources(ordered):
        lanes = [None] * fanout
        for beside in reversed(range(fanout)):
            lanes[beside] = [
                send(ordered[other], lambda layer, lane, col: (layer, (lane - beside) % fanout, col ^ other))
                if beside or other
                else ordered[0]
                for other in range(cols_count)
            ]
        return lanes

    chunks = split_waves(history.shape[2])
    half = history.shape[1] // 2
    moving = [(history[:, :half, start:stop], history[:, half:, start:stop]) for start, stop in chunks]
    carried, marks = [None] * len(chunks), [None] * len(chunks)
    arrived = [[moving[number]] for number in range(len(chunks))]

    def add_piece(number, step):
        start, stop = chunks[number]
        outs = past_call(
            delay,
            tile,
            interaction,
            arrived[number][step],
            marks[number],
            carried[number],
            None,
            step,
            (0, 1),
            layers,
            fanout,
        )
        carried[number], marks[number] = outs

    marks = [mark] * len(chunks)
    added = [0] * len(chunks)
    for step in range(1, rows_count):
        for number in range(len(chunks)):
            front, back = arrived[number][-1]
            if step >= 2 and aligned:
                wanted = 0 if step == 2 else 1 if step == 3 else step - 1
                while added[number] < wanted:
                    add_piece(number, added[number])
                    added[number] += 1
                front, back, marks[number] = lax.optimization_barrier((front, back, marks[number]))
            arrived[number].append((around(front, 1), around(back, -1)))
    last = rows_count - 1
    for number, (start, stop) in enumerate(chunks):
        if aligned:
            for step in range(added[number], last):
                add_piece(number, step)
            arrived[number] = arrived[number][last]
        else:
            fronts, backs = zip(*arrived[number])
            ordered = jnp.stack([in_row_order(fronts, 1), in_row_order(backs, -1)], axis=1)
            ordered = jnp.moveaxis(ordered, 2, 0).reshape(history.shape[0], 2, rows_count * half, stop - start)
            arrived[number] = ordered[:, 0], ordered[:, 1]

    def end_past(number, step):
        start, stop = chunks[number]
        return past_call(
            delay,
            tile,
            interaction,
            arrived[number],
            marks[number],
            carried[number],
            incident[:, :, start:stop],
            last,
            (step,),
            layers,
            fanout,
        )

    numbers = range(len(chunks))
    kepts, sents = [None] * len(chunks), [None] * len(chunks)
    for number in numbers:
        kepts[number], sents[number] = folded(*end_past(number, 0))
    gots, laters = [], []
    for number in numbers:
        gots.append(last_hop(sents[number]))
        sents[number], marks[number] = lax.optimization_barrier((sents[number], marks[number]))
        laters.append(end_past(number, 1)[0])
    by_layers = [to_layers(load_call(interaction, kepts[number], gots[number], gain, cubic)) for number in numbers]
    every, ends = [], []
    for number in numbers:
        ordered = arrange_call(interaction, [by_layers[number][apart] for apart in range(layers)], fanout)
        if number:
            ordered, ends[-1] = lax.optimization_barrier((ordered, ends[-1]))
        every.append(to_sources(ordered))
        ends.append(
            recent_call(delay, tile, interaction, every[number][0], laters[number], 0, fanout, cols_count)
        )
    for number in numbers:
        for beside in range(1, fanout):
            ends[number] = recent_call(
                delay, tile, interaction, every[number][beside], ends[number][0], beside, fanout, cols_count
            )
        kepts[number], sents[number] = folded(*ends[number])
    gots = [last_hop(sents[number]) for number in numbers]
    lasts = [load_call(interaction, kepts[number], gots[number], gain, cubic) for number in numbers]
    results = [jnp.stack([by_layer[0], last]) for by_layer, last in zip(by_layers, lasts)]
    return jnp.concatenate(results, axis=2)


def solution(mesh):
    placed = (
        P(None, "row", "col"),
        P(None, ("col", "row"), None),
        P(None, ("row", "col"), None),
        P("row"),
        P("row"),
        P("row", "col", None),
        P("row", "col"),
    )
    return jax.shard_map(
        functools.partial(per_device, mesh.shape["row"], mesh.shape["col"]),
        mesh=mesh,
        in_specs=placed,
        out_specs=P(None, ("row", "col"), None),
        check_vma=False,
    )
```

```python
import functools

import jax
import jax.numpy as jnp
from jax import lax
from jax.experimental import pallas as pl
from jax.experimental.pallas import tpu as pltpu
from jax.sharding import PartitionSpec as P

BOTH = ("row", "col")
VMEM_BYTES = 8 * 1024 * 1024
TILE = 16
ROWS = 512
SHORT = pl.CostEstimate(flops=0, bytes_accessed=0, transcendentals=0)
LANES = 128
LEVELS = 32000.0
IN_VMEM = pl.BlockSpec(memory_space=pltpu.VMEM)
IN_SMEM = pl.BlockSpec(memory_space=pltpu.SMEM)


def split_waves(waves):
    unit = 128
    if waves % unit or waves < 2 * unit:
        return [(0, waves)]
    half = (waves // unit + 1) // 2 * unit
    return [(0, half), (half, waves)]


def whereabouts(fanout):
    row = lax.axis_index("row")
    return lax.div(row, fanout), lax.rem(row, fanout), lax.axis_index("col")


def cycle_row(layers, fanout, place):
    lane, along = lax.div(place, layers), lax.rem(place, layers)
    return jnp.where(lax.rem(lane, 2) == 0, along, layers - 1 - along) * fanout + lane


def cycle_place(layers, layer, lane):
    return lane * layers + jnp.where(lax.rem(lane, 2) == 0, layer, layers - 1 - layer)


def first_kernel(matrix, gain, cubic, mark, own_gain, own_cubic, held):
    mark[...] = matrix[0, :8, :128].astype(jnp.float32)
    share = own_gain.shape[0]
    own = pl.ds(pl.multiple_of(lax.axis_index("col") * share, share), share)
    for source, out in ((gain, own_gain), (cubic, own_cubic)):
        for number in range(source.shape[0]):
            line = jnp.broadcast_to(source[number : number + 1, :], (LANES, LANES))
            held[number * LANES : (number + 1) * LANES, :] = jnp.transpose(line)
        out[...] = held[own, :]


def first_call(matrix, gain, cubic, share):
    rows = matrix.shape[1]
    lines = (rows // LANES, LANES)
    return pl.pallas_call(
        first_kernel,
        out_shape=[jax.ShapeDtypeStruct((8, LANES), jnp.float32)]
        + [jax.ShapeDtypeStruct((share, LANES), jnp.float32)] * 2,
        in_specs=[IN_VMEM] * 3,
        out_specs=[IN_VMEM] * 3,
        scratch_shapes=[pltpu.VMEM((rows, LANES), jnp.float32)],
        compiler_params=pltpu.CompilerParams(vmem_limit_bytes=VMEM_BYTES),
        cost_estimate=SHORT,
    )(matrix, gain.reshape(lines), cubic.reshape(lines))


def past_kernel(number, opening, steps, layers, fanout, delays, tile, matrix, front, back, mark, *refs):
    refs = list(refs)
    carried = None if opening else refs.pop(0)
    incident = refs.pop(0) if len(steps) == 1 else None
    slots = matrix.shape[0]
    depth, half, waves = front.shape
    layer, lane, col = whereabouts(fanout)
    count = matrix.shape[2] // (2 * half)
    here = cycle_place(layers, layer, lane)
    right, columns = [], []
    for side, piece in enumerate((front, back)):
        if count == 1:
            place = side
        else:
            walked = lax.rem(here + (number if side else count - number), count)
            place = 2 * cycle_row(layers, fanout, walked) + side
        columns.append(pl.ds(pl.multiple_of(place * half, half), half))
        for slot in range(slots):
            delay = delays[slot]
            parts = []
            if 0 in steps:
                parts.append(piece[depth - delay])
            if 1 in steps:
                later = piece[jnp.minimum(depth + 1 - delay, depth - 1)]
                parts.append(jnp.where(delay >= 2, later, jnp.zeros_like(later)))
            right.append(jnp.concatenate(parts, axis=1))
    right = jnp.concatenate(right, axis=0)
    span = slice(None) if len(steps) == 2 else slice(steps[0] * waves, (steps[0] + 1) * waves)
    total = refs[-1] if steps == (0,) else refs[0]
    weight = 1.0 if len(steps) == 2 else -tile[0].astype(jnp.float32)

    def some_rows(turn, _):
        rows = pl.ds(pl.multiple_of(turn * ROWS, ROWS), ROWS)
        left = jnp.concatenate([matrix[slot, rows, line] for line in columns for slot in range(slots)], axis=1)
        added = jnp.dot(left, right, preferred_element_type=jnp.float32)
        if not opening:
            added = added + carried[rows, span]
        total[rows, :] = added if len(steps) == 2 else weight * added
        return 0

    lax.fori_loop(0, matrix.shape[1] // ROWS, some_rows, 0)
    if len(steps) == 2:
        refs[1][...] = jnp.zeros_like(refs[1])
        return
    share = incident.shape[1]
    if steps[0]:
        total[pl.ds(pl.multiple_of(col * share, share), share), :] += incident[1]
        return
    kept, sent, held = refs
    bit = lax.rem(col, 2)
    for pair in range(kept.shape[0]):
        for out, which in ((kept, bit), (sent, 1 - bit)):
            rows = pl.ds(pl.multiple_of((2 * pair + which) * share, share), share)
            out[pair] = held[rows, :]
    kept[lax.div(col, 2)] += incident[0]


def past_call(delays, tile, matrix, pieces, mark, carried, incident, number, steps, layers, fanout):
    slots, rows, _ = matrix.shape
    _, half, waves = pieces[0].shape
    totals = jax.ShapeDtypeStruct((rows, 2 * waves), jnp.float32)
    operands = [delays, tile, matrix, *pieces, mark]
    aliases, scratch = {}, []
    if carried is not None:
        operands.append(carried)
    if len(steps) == 2:
        ends = [totals, jax.ShapeDtypeStruct((8, LANES), jnp.float32)]
        aliases = {} if carried is None else {6: 0}
    else:
        operands.append(incident)
        share = incident.shape[1]
        if steps[0]:
            ends = [jax.ShapeDtypeStruct((rows, waves), jnp.float32)]
        else:
            ends = [jax.ShapeDtypeStruct((rows // share // 2, share, waves), jnp.float32)] * 2
            scratch = [pltpu.VMEM((rows, waves), jnp.float32)]
    return pl.pallas_call(
        functools.partial(past_kernel, number, carried is None, steps, layers, fanout),
        out_shape=ends,
        in_specs=[IN_SMEM] * 2 + [IN_VMEM] * (len(operands) - 2),
        out_specs=[IN_VMEM] * len(ends),
        scratch_shapes=scratch,
        input_output_aliases=aliases,
        compiler_params=pltpu.CompilerParams(vmem_limit_bytes=VMEM_BYTES),
        cost_estimate=pl.CostEstimate(
            flops=4 * slots * rows * half * waves * len(steps),
            bytes_accessed=4 * slots * rows * half,
            transcendentals=0,
        ),
    )(*operands)


def small_call(kernel, shapes, matrix, *operands):
    return pl.pallas_call(
        kernel,
        out_shape=shapes,
        in_specs=[IN_VMEM] * (1 + len(operands)),
        out_specs=[IN_VMEM] * len(shapes),
        compiler_params=pltpu.CompilerParams(vmem_limit_bytes=VMEM_BYTES),
        cost_estimate=SHORT,
    )(matrix, *operands)


def fold_kernel(bit, last, matrix, kept, got, kept_out, sent_out):
    own = lax.rem(lax.div(lax.axis_index("col"), bit), 2)
    for pair in range(kept_out.shape[0]):
        kept_out[pair] = kept[2 * pair + own] + got[2 * pair + own]
        sent = kept[2 * pair + 1 - own] + got[2 * pair + 1 - own]
        if not last:
            sent_out[pair] = sent
            continue
        rows = sent.shape[0]
        peak = jnp.maximum(jnp.max(jnp.abs(sent), axis=0, keepdims=True), 1e-30)
        power = jnp.ceil(jnp.log2(peak))
        coded = jnp.round(sent * (jnp.exp2(-power) * LEVELS))
        sent_out[:rows] = coded.astype(jnp.int32).astype(jnp.int16)
        sent_out[rows:] = jnp.broadcast_to(power, (TILE, sent.shape[1])).astype(jnp.int32).astype(jnp.int16)


def fold_call(matrix, kept, got, bit, last):
    pairs, (share, waves) = kept.shape[0] // 2, kept.shape[1:]
    shapes = [jax.ShapeDtypeStruct((pairs, share, waves), jnp.float32)]
    if last:
        shapes.append(jax.ShapeDtypeStruct((share + TILE, waves), jnp.int16))
    else:
        shapes.append(shapes[0])
    return small_call(functools.partial(fold_kernel, bit, last), shapes, matrix, kept, got)


def load_kernel(matrix, kept, got, gain, cubic, out):
    share, waves = out.shape
    gain, cubic = (jnp.concatenate([ref[...]] * (waves // LANES), axis=1) for ref in (gain, cubic))
    power = got[share:].astype(jnp.int32).astype(jnp.float32)[:1]
    field = kept[0] + got[:share].astype(jnp.int32).astype(jnp.float32) * (jnp.exp2(power) * (1.0 / LEVELS))
    out[...] = (gain * field - cubic * field * field * field).astype(jnp.bfloat16)


def load_call(matrix, kept, got, gain, cubic):
    shapes = [jax.ShapeDtypeStruct(kept.shape[1:], jnp.bfloat16)]
    return small_call(load_kernel, shapes, matrix, kept, got, gain, cubic)[0]


def arrange_kernel(layers, fanout, matrix, *refs):
    layer, _, col = whereabouts(fanout)
    apart = layer ^ col
    for place in range(layers):
        @pl.when(apart == place)
        def _():
            for other in range(layers):
                refs[layers + other][...] = refs[place ^ other][...]


def arrange_call(matrix, values, fanout):
    shapes = [jax.ShapeDtypeStruct(value.shape, value.dtype) for value in values]
    return small_call(functools.partial(arrange_kernel, len(values), fanout), shapes, matrix, *values)


def recent_kernel(fanout, beside, ending, pieces, delays, tile, matrix, *refs):
    sources, base, refs = refs[:pieces], refs[pieces], list(refs[pieces + 1 :])
    outs = [refs.pop(0) for _ in range(2 if ending else 1)]
    total, held = refs
    slots = matrix.shape[0]
    _, lane, col = whereabouts(fanout)
    depth, share = held.shape[0], sources[0].shape[0]
    for other, source in enumerate(sources):
        held[pl.ds(pl.multiple_of((col ^ other) * share, share), share), :] = source[...]
    lane = lax.rem(lane + beside, fanout)
    columns = pl.ds(pl.multiple_of(lane * depth, depth), depth)
    total[...] = jnp.zeros_like(total)

    def some_slot(slot, _):
        @pl.when(delays[slot] == 1)
        def _():
            total[...] += jnp.dot(matrix[slot, :, columns], held[...], preferred_element_type=jnp.float32)

        return 0

    lax.fori_loop(0, slots, some_slot, 0)
    weight = -tile[0].astype(jnp.float32)
    if not ending:
        outs[0][...] = base[...] + weight * total[...]
        return
    bit = lax.rem(col, 2)
    for pair in range(outs[0].shape[0]):
        for out, own in ((outs[0], bit), (outs[1], 1 - bit)):
            rows = pl.ds(pl.multiple_of((2 * pair + own) * share, share), share)
            out[pair] = base[rows, :] + weight * total[rows, :]


def recent_call(delays, tile, matrix, sources, base, beside, fanout, cols_count):
    slots, rows, depth = matrix.shape
    waves = base.shape[1]
    depth = depth // fanout
    ending = beside == fanout - 1
    if ending:
        ends = [jax.ShapeDtypeStruct((cols_count // 2, rows // cols_count, waves), jnp.float32)] * 2
    else:
        ends = [jax.ShapeDtypeStruct(base.shape, jnp.float32)]
    return pl.pallas_call(
        functools.partial(recent_kernel, fanout, beside, ending, len(sources)),
        out_shape=ends,
        in_specs=[IN_SMEM] * 2 + [IN_VMEM] * (len(sources) + 2),
        out_specs=[IN_VMEM] * len(ends),
        scratch_shapes=[pltpu.VMEM((rows, waves), jnp.float32), pltpu.VMEM((depth, waves), jnp.bfloat16)],
        compiler_params=pltpu.CompilerParams(vmem_limit_bytes=VMEM_BYTES),
        cost_estimate=SHORT,
    )(delays, tile, matrix, *sources, base)


def per_device(rows_count, cols_count, interaction, history, incident, load_gain, load_cubic, delays, tile_map):
    fanout = rows_count // cols_count
    layers = cols_count
    share = incident.shape[1]
    delay, tile = delays.reshape(-1), tile_map.reshape(-1)
    bits = [1 << bit for bit in range((cols_count - 1).bit_length())]

    def send(value, target):
        pairs = []
        for row in range(rows_count):
            for col in range(cols_count):
                goal = target(row // fanout, row % fanout, col)
                if goal is not None:
                    pairs.append((row * cols_count + col, (goal[0] * fanout + goal[1]) * cols_count + goal[2]))
        return lax.ppermute(value, BOTH, pairs)

    cycle = [
        (layer if lane % 2 == 0 else layers - 1 - layer) * fanout + lane
        for lane in range(fanout)
        for layer in range(layers)
    ]
    spot = {row: place for place, row in enumerate(cycle)}

    def around(value, steps):
        pairs = [(row, cycle[(spot[row] + steps) % rows_count]) for row in range(rows_count)]
        return lax.ppermute(value, "row", pairs)

    aligned = history.shape[1] % 256 == 0

    def in_row_order(values, sense):
        row = lax.axis_index("row")
        here = jnp.asarray([spot[row] for row in range(rows_count)], jnp.int32)[row]
        rows = jnp.asarray(cycle, jnp.int32)[(here - sense * jnp.arange(rows_count)) % rows_count]
        return jnp.take(jnp.stack(values), jnp.argsort(rows), axis=0)

    mark, gain, cubic = first_call(interaction, load_gain, load_cubic, share)

    def folded(kept, sent):
        for bit in bits[:-1]:
            got = send(sent, lambda layer, lane, col: (layer, lane, col ^ bit))
            kept, sent = fold_call(interaction, kept, got, 2 * bit, 2 * bit == bits[-1])
        return kept, sent

    def last_hop(sent):
        return send(sent, lambda layer, lane, col: (layer, lane, col ^ bits[-1]))

    def to_layers(current):
        by_layer = {0: current}
        for bit in reversed(bits):
            for apart in list(by_layer):
                value = by_layer[apart]
                if apart and bit in by_layer:
                    value, by_layer[bit] = lax.optimization_barrier((value, by_layer[bit]))
                by_layer[apart ^ bit] = send(value, lambda layer, lane, col: (layer ^ bit, lane, col))
        return by_layer

    def to_sources(ordered):
        lanes = [None] * fanout
        for beside in reversed(range(fanout)):
            lanes[beside] = [
                send(ordered[other], lambda layer, lane, col: (layer, (lane - beside) % fanout, col ^ other))
                if beside or other
                else ordered[0]
                for other in range(cols_count)
            ]
        return lanes

    chunks = split_waves(history.shape[2])
    half = history.shape[1] // 2
    moving = [(history[:, :half, start:stop], history[:, half:, start:stop]) for start, stop in chunks]
    carried, marks = [None] * len(chunks), [None] * len(chunks)
    arrived = [[moving[number]] for number in range(len(chunks))]

    def add_piece(number, step):
        start, stop = chunks[number]
        outs = past_call(
            delay,
            tile,
            interaction,
            arrived[number][step],
            marks[number],
            carried[number],
            None,
            step,
            (0, 1),
            layers,
            fanout,
        )
        carried[number], marks[number] = outs

    marks = [mark] * len(chunks)
    added = [0] * len(chunks)
    for step in range(1, rows_count):
        for number in range(len(chunks)):
            front, back = arrived[number][-1]
            if step >= 2 and aligned:
                wanted = 0 if step == 2 else 1 if step == 3 else step - 1
                while added[number] < wanted:
                    add_piece(number, added[number])
                    added[number] += 1
                front, back, marks[number] = lax.optimization_barrier((front, back, marks[number]))
            arrived[number].append((around(front, 1), around(back, -1)))
    last = rows_count - 1
    for number, (start, stop) in enumerate(chunks):
        if aligned:
            for step in range(added[number], last):
                add_piece(number, step)
            arrived[number] = arrived[number][last]
        else:
            fronts, backs = zip(*arrived[number])
            ordered = jnp.stack([in_row_order(fronts, 1), in_row_order(backs, -1)], axis=1)
            ordered = jnp.moveaxis(ordered, 2, 0).reshape(history.shape[0], 2, rows_count * half, stop - start)
            arrived[number] = ordered[:, 0], ordered[:, 1]

    def end_past(number, step):
        start, stop = chunks[number]
        return past_call(
            delay,
            tile,
            interaction,
            arrived[number],
            marks[number],
            carried[number],
            incident[:, :, start:stop],
            last,
            (step,),
            layers,
            fanout,
        )

    numbers = range(len(chunks))
    kepts, sents = [None] * len(chunks), [None] * len(chunks)
    for number in numbers:
        kepts[number], sents[number] = folded(*end_past(number, 0))
    gots, laters = [], []
    for number in numbers:
        gots.append(last_hop(sents[number]))
        sents[number], marks[number] = lax.optimization_barrier((sents[number], marks[number]))
        later, gots[number] = lax.optimization_barrier((end_past(number, 1)[0], gots[number]))
        laters.append(later)
    by_layers = [to_layers(load_call(interaction, kepts[number], gots[number], gain, cubic)) for number in numbers]
    every, ends = [], []
    for number in numbers:
        ordered = arrange_call(interaction, [by_layers[number][apart] for apart in range(layers)], fanout)
        if number:
            ordered, ends[-1] = lax.optimization_barrier((ordered, ends[-1]))
        every.append(to_sources(ordered))
        ends.append(
            recent_call(delay, tile, interaction, every[number][0], laters[number], 0, fanout, cols_count)
        )
    for number in numbers:
        for beside in range(1, fanout):
            ends[number] = recent_call(
                delay, tile, interaction, every[number][beside], ends[number][0], beside, fanout, cols_count
            )
        kepts[number], sents[number] = folded(*ends[number])
    gots = [last_hop(sents[number]) for number in numbers]
    lasts = [load_call(interaction, kepts[number], gots[number], gain, cubic) for number in numbers]
    results = [jnp.stack([by_layer[0], last]) for by_layer, last in zip(by_layers, lasts)]
    return jnp.concatenate(results, axis=2)


def solution(mesh):
    placed = (
        P(None, "row", "col"),
        P(None, ("col", "row"), None),
        P(None, ("row", "col"), None),
        P("row"),
        P("row"),
        P("row", "col", None),
        P("row", "col"),
    )
    return jax.shard_map(
        functools.partial(per_device, mesh.shape["row"], mesh.shape["col"]),
        mesh=mesh,
        in_specs=placed,
        out_specs=P(None, ("row", "col"), None),
        check_vma=False,
    )
```

```python
import functools

import jax
import jax.numpy as jnp
from jax import lax
from jax.experimental import pallas as pl
from jax.experimental.pallas import tpu as pltpu
from jax.sharding import PartitionSpec as P

BOTH = ("row", "col")
VMEM_BYTES = 8 * 1024 * 1024
TILE = 16
ROWS = 512
SHORT = pl.CostEstimate(flops=0, bytes_accessed=0, transcendentals=0)
LANES = 128
LEVELS = 32000.0
IN_VMEM = pl.BlockSpec(memory_space=pltpu.VMEM)
IN_SMEM = pl.BlockSpec(memory_space=pltpu.SMEM)


def split_waves(waves):
    unit = 128
    if waves % unit or waves < 2 * unit:
        return [(0, waves)]
    half = (waves // unit + 1) // 2 * unit
    return [(0, half), (half, waves)]


def whereabouts(fanout):
    row = lax.axis_index("row")
    return lax.div(row, fanout), lax.rem(row, fanout), lax.axis_index("col")


def cycle_row(layers, fanout, place):
    lane, along = lax.div(place, layers), lax.rem(place, layers)
    return jnp.where(lax.rem(lane, 2) == 0, along, layers - 1 - along) * fanout + lane


def cycle_place(layers, layer, lane):
    return lane * layers + jnp.where(lax.rem(lane, 2) == 0, layer, layers - 1 - layer)


def first_kernel(matrix, gain, cubic, mark, own_gain, own_cubic, held):
    mark[...] = matrix[0, :8, :128].astype(jnp.float32)
    share = own_gain.shape[0]
    own = pl.ds(pl.multiple_of(lax.axis_index("col") * share, share), share)
    for source, out in ((gain, own_gain), (cubic, own_cubic)):
        for number in range(source.shape[0]):
            line = jnp.broadcast_to(source[number : number + 1, :], (LANES, LANES))
            held[number * LANES : (number + 1) * LANES, :] = jnp.transpose(line)
        out[...] = held[own, :]


def first_call(matrix, gain, cubic, share):
    rows = matrix.shape[1]
    lines = (rows // LANES, LANES)
    return pl.pallas_call(
        first_kernel,
        out_shape=[jax.ShapeDtypeStruct((8, LANES), jnp.float32)]
        + [jax.ShapeDtypeStruct((share, LANES), jnp.float32)] * 2,
        in_specs=[IN_VMEM] * 3,
        out_specs=[IN_VMEM] * 3,
        scratch_shapes=[pltpu.VMEM((rows, LANES), jnp.float32)],
        compiler_params=pltpu.CompilerParams(vmem_limit_bytes=VMEM_BYTES),
        cost_estimate=SHORT,
    )(matrix, gain.reshape(lines), cubic.reshape(lines))


def past_kernel(number, opening, steps, layers, fanout, delays, tile, matrix, front, back, mark, *refs):
    refs = list(refs)
    carried = None if opening else refs.pop(0)
    incident = refs.pop(0) if len(steps) == 1 else None
    slots = matrix.shape[0]
    depth, half, waves = front.shape
    layer, lane, col = whereabouts(fanout)
    count = matrix.shape[2] // (2 * half)
    here = cycle_place(layers, layer, lane)
    right, columns = [], []
    for side, piece in enumerate((front, back)):
        if count == 1:
            place = side
        else:
            walked = lax.rem(here + (number if side else count - number), count)
            place = 2 * cycle_row(layers, fanout, walked) + side
        columns.append(pl.ds(pl.multiple_of(place * half, half), half))
        for slot in range(slots):
            delay = delays[slot]
            parts = []
            if 0 in steps:
                parts.append(piece[depth - delay])
            if 1 in steps:
                later = piece[jnp.minimum(depth + 1 - delay, depth - 1)]
                parts.append(jnp.where(delay >= 2, later, jnp.zeros_like(later)))
            right.append(jnp.concatenate(parts, axis=1))
    right = jnp.concatenate(right, axis=0)
    span = slice(None) if len(steps) == 2 else slice(steps[0] * waves, (steps[0] + 1) * waves)
    total = refs[-1] if steps == (0,) else refs[0]
    weight = 1.0 if len(steps) == 2 else -tile[0].astype(jnp.float32)

    height = matrix.shape[1] if 1 < count <= number + 2 else ROWS

    def some_rows(turn, _):
        rows = pl.ds(pl.multiple_of(turn * height, height), height)
        left = jnp.concatenate([matrix[slot, rows, line] for line in columns for slot in range(slots)], axis=1)
        added = jnp.dot(left, right, preferred_element_type=jnp.float32)
        if not opening:
            added = added + carried[rows, span]
        total[rows, :] = added if len(steps) == 2 else weight * added
        return 0

    lax.fori_loop(0, matrix.shape[1] // height, some_rows, 0)
    if len(steps) == 2:
        refs[1][...] = jnp.zeros_like(refs[1])
        return
    share = incident.shape[1]
    if steps[0]:
        total[pl.ds(pl.multiple_of(col * share, share), share), :] += incident[1]
        return
    kept, sent, held = refs
    bit = lax.rem(col, 2)
    for pair in range(kept.shape[0]):
        for out, which in ((kept, bit), (sent, 1 - bit)):
            rows = pl.ds(pl.multiple_of((2 * pair + which) * share, share), share)
            out[pair] = held[rows, :]
    kept[lax.div(col, 2)] += incident[0]


def past_call(delays, tile, matrix, pieces, mark, carried, incident, number, steps, layers, fanout):
    slots, rows, _ = matrix.shape
    _, half, waves = pieces[0].shape
    totals = jax.ShapeDtypeStruct((rows, 2 * waves), jnp.float32)
    operands = [delays, tile, matrix, *pieces, mark]
    aliases, scratch = {}, []
    if carried is not None:
        operands.append(carried)
    if len(steps) == 2:
        ends = [totals, jax.ShapeDtypeStruct((8, LANES), jnp.float32)]
        aliases = {} if carried is None else {6: 0}
    else:
        operands.append(incident)
        share = incident.shape[1]
        if steps[0]:
            ends = [jax.ShapeDtypeStruct((rows, waves), jnp.float32)]
        else:
            ends = [jax.ShapeDtypeStruct((rows // share // 2, share, waves), jnp.float32)] * 2
            scratch = [pltpu.VMEM((rows, waves), jnp.float32)]
    return pl.pallas_call(
        functools.partial(past_kernel, number, carried is None, steps, layers, fanout),
        out_shape=ends,
        in_specs=[IN_SMEM] * 2 + [IN_VMEM] * (len(operands) - 2),
        out_specs=[IN_VMEM] * len(ends),
        scratch_shapes=scratch,
        input_output_aliases=aliases,
        compiler_params=pltpu.CompilerParams(vmem_limit_bytes=VMEM_BYTES),
        cost_estimate=pl.CostEstimate(
            flops=4 * slots * rows * half * waves * len(steps),
            bytes_accessed=4 * slots * rows * half,
            transcendentals=0,
        ),
    )(*operands)


def small_call(kernel, shapes, matrix, *operands):
    return pl.pallas_call(
        kernel,
        out_shape=shapes,
        in_specs=[IN_VMEM] * (1 + len(operands)),
        out_specs=[IN_VMEM] * len(shapes),
        compiler_params=pltpu.CompilerParams(vmem_limit_bytes=VMEM_BYTES),
        cost_estimate=SHORT,
    )(matrix, *operands)


def fold_kernel(bit, last, matrix, kept, got, kept_out, sent_out):
    own = lax.rem(lax.div(lax.axis_index("col"), bit), 2)
    for pair in range(kept_out.shape[0]):
        kept_out[pair] = kept[2 * pair + own] + got[2 * pair + own]
        sent = kept[2 * pair + 1 - own] + got[2 * pair + 1 - own]
        if not last:
            sent_out[pair] = sent
            continue
        rows = sent.shape[0]
        peak = jnp.maximum(jnp.max(jnp.abs(sent), axis=0, keepdims=True), 1e-30)
        power = jnp.ceil(jnp.log2(peak))
        coded = jnp.round(sent * (jnp.exp2(-power) * LEVELS))
        sent_out[:rows] = coded.astype(jnp.int32).astype(jnp.int16)
        sent_out[rows:] = jnp.broadcast_to(power, (TILE, sent.shape[1])).astype(jnp.int32).astype(jnp.int16)


def fold_call(matrix, kept, got, bit, last):
    pairs, (share, waves) = kept.shape[0] // 2, kept.shape[1:]
    shapes = [jax.ShapeDtypeStruct((pairs, share, waves), jnp.float32)]
    if last:
        shapes.append(jax.ShapeDtypeStruct((share + TILE, waves), jnp.int16))
    else:
        shapes.append(shapes[0])
    return small_call(functools.partial(fold_kernel, bit, last), shapes, matrix, kept, got)


def load_kernel(matrix, kept, got, gain, cubic, out):
    share, waves = out.shape
    gain, cubic = (jnp.concatenate([ref[...]] * (waves // LANES), axis=1) for ref in (gain, cubic))
    power = got[share:].astype(jnp.int32).astype(jnp.float32)[:1]
    field = kept[0] + got[:share].astype(jnp.int32).astype(jnp.float32) * (jnp.exp2(power) * (1.0 / LEVELS))
    out[...] = (gain * field - cubic * field * field * field).astype(jnp.bfloat16)


def load_call(matrix, kept, got, gain, cubic):
    shapes = [jax.ShapeDtypeStruct(kept.shape[1:], jnp.bfloat16)]
    return small_call(load_kernel, shapes, matrix, kept, got, gain, cubic)[0]


def arrange_kernel(layers, fanout, matrix, *refs):
    layer, _, col = whereabouts(fanout)
    apart = layer ^ col
    for place in range(layers):
        @pl.when(apart == place)
        def _():
            for other in range(layers):
                refs[layers + other][...] = refs[place ^ other][...]


def arrange_call(matrix, values, fanout):
    shapes = [jax.ShapeDtypeStruct(value.shape, value.dtype) for value in values]
    return small_call(functools.partial(arrange_kernel, len(values), fanout), shapes, matrix, *values)


def recent_kernel(fanout, beside, ending, pieces, delays, tile, matrix, *refs):
    sources, base, refs = refs[:pieces], refs[pieces], list(refs[pieces + 1 :])
    outs = [refs.pop(0) for _ in range(2 if ending else 1)]
    total, held = refs
    slots = matrix.shape[0]
    _, lane, col = whereabouts(fanout)
    depth, share = held.shape[0], sources[0].shape[0]
    for other, source in enumerate(sources):
        held[pl.ds(pl.multiple_of((col ^ other) * share, share), share), :] = source[...]
    lane = lax.rem(lane + beside, fanout)
    columns = pl.ds(pl.multiple_of(lane * depth, depth), depth)
    total[...] = jnp.zeros_like(total)

    def some_slot(slot, _):
        @pl.when(delays[slot] == 1)
        def _():
            total[...] += jnp.dot(matrix[slot, :, columns], held[...], preferred_element_type=jnp.float32)

        return 0

    lax.fori_loop(0, slots, some_slot, 0)
    weight = -tile[0].astype(jnp.float32)
    if not ending:
        outs[0][...] = base[...] + weight * total[...]
        return
    bit = lax.rem(col, 2)
    for pair in range(outs[0].shape[0]):
        for out, own in ((outs[0], bit), (outs[1], 1 - bit)):
            rows = pl.ds(pl.multiple_of((2 * pair + own) * share, share), share)
            out[pair] = base[rows, :] + weight * total[rows, :]


def recent_call(delays, tile, matrix, sources, base, beside, fanout, cols_count):
    slots, rows, depth = matrix.shape
    waves = base.shape[1]
    depth = depth // fanout
    ending = beside == fanout - 1
    if ending:
        ends = [jax.ShapeDtypeStruct((cols_count // 2, rows // cols_count, waves), jnp.float32)] * 2
    else:
        ends = [jax.ShapeDtypeStruct(base.shape, jnp.float32)]
    return pl.pallas_call(
        functools.partial(recent_kernel, fanout, beside, ending, len(sources)),
        out_shape=ends,
        in_specs=[IN_SMEM] * 2 + [IN_VMEM] * (len(sources) + 2),
        out_specs=[IN_VMEM] * len(ends),
        scratch_shapes=[pltpu.VMEM((rows, waves), jnp.float32), pltpu.VMEM((depth, waves), jnp.bfloat16)],
        compiler_params=pltpu.CompilerParams(vmem_limit_bytes=VMEM_BYTES),
        cost_estimate=SHORT,
    )(delays, tile, matrix, *sources, base)


def per_device(rows_count, cols_count, interaction, history, incident, load_gain, load_cubic, delays, tile_map):
    fanout = rows_count // cols_count
    layers = cols_count
    share = incident.shape[1]
    delay, tile = delays.reshape(-1), tile_map.reshape(-1)
    bits = [1 << bit for bit in range((cols_count - 1).bit_length())]

    def send(value, target):
        pairs = []
        for row in range(rows_count):
            for col in range(cols_count):
                goal = target(row // fanout, row % fanout, col)
                if goal is not None:
                    pairs.append((row * cols_count + col, (goal[0] * fanout + goal[1]) * cols_count + goal[2]))
        return lax.ppermute(value, BOTH, pairs)

    cycle = [
        (layer if lane % 2 == 0 else layers - 1 - layer) * fanout + lane
        for lane in range(fanout)
        for layer in range(layers)
    ]
    spot = {row: place for place, row in enumerate(cycle)}

    def around(value, steps):
        pairs = [(row, cycle[(spot[row] + steps) % rows_count]) for row in range(rows_count)]
        return lax.ppermute(value, "row", pairs)

    aligned = history.shape[1] % 256 == 0

    def in_row_order(values, sense):
        row = lax.axis_index("row")
        here = jnp.asarray([spot[row] for row in range(rows_count)], jnp.int32)[row]
        rows = jnp.asarray(cycle, jnp.int32)[(here - sense * jnp.arange(rows_count)) % rows_count]
        return jnp.take(jnp.stack(values), jnp.argsort(rows), axis=0)

    mark, gain, cubic = first_call(interaction, load_gain, load_cubic, share)

    def folded(kept, sent):
        for bit in bits[:-1]:
            got = send(sent, lambda layer, lane, col: (layer, lane, col ^ bit))
            kept, sent = fold_call(interaction, kept, got, 2 * bit, 2 * bit == bits[-1])
        return kept, sent

    def last_hop(sent):
        return send(sent, lambda layer, lane, col: (layer, lane, col ^ bits[-1]))

    def to_layers(current):
        by_layer = {0: current}
        for bit in reversed(bits):
            for apart in list(by_layer):
                value = by_layer[apart]
                if apart and bit in by_layer:
                    value, by_layer[bit] = lax.optimization_barrier((value, by_layer[bit]))
                by_layer[apart ^ bit] = send(value, lambda layer, lane, col: (layer ^ bit, lane, col))
        return by_layer

    def to_sources(ordered):
        lanes = [None] * fanout
        for beside in reversed(range(fanout)):
            lanes[beside] = [
                send(ordered[other], lambda layer, lane, col: (layer, (lane - beside) % fanout, col ^ other))
                if beside or other
                else ordered[0]
                for other in range(cols_count)
            ]
        return lanes

    chunks = split_waves(history.shape[2])
    half = history.shape[1] // 2
    moving = [(history[:, :half, start:stop], history[:, half:, start:stop]) for start, stop in chunks]
    carried, marks = [None] * len(chunks), [None] * len(chunks)
    arrived = [[moving[number]] for number in range(len(chunks))]

    def add_piece(number, step):
        start, stop = chunks[number]
        outs = past_call(
            delay,
            tile,
            interaction,
            arrived[number][step],
            marks[number],
            carried[number],
            None,
            step,
            (0, 1),
            layers,
            fanout,
        )
        carried[number], marks[number] = outs

    marks = [mark] * len(chunks)
    added = [0] * len(chunks)
    for step in range(1, rows_count):
        for number in range(len(chunks)):
            front, back = arrived[number][-1]
            if step >= 2 and aligned:
                wanted = 0 if step == 2 else 1 if step == 3 else step - 1
                while added[number] < wanted:
                    add_piece(number, added[number])
                    added[number] += 1
                front, back, marks[number] = lax.optimization_barrier((front, back, marks[number]))
            arrived[number].append((around(front, 1), around(back, -1)))
    last = rows_count - 1
    for number, (start, stop) in enumerate(chunks):
        if aligned:
            for step in range(added[number], last):
                add_piece(number, step)
            arrived[number] = arrived[number][last]
        else:
            fronts, backs = zip(*arrived[number])
            ordered = jnp.stack([in_row_order(fronts, 1), in_row_order(backs, -1)], axis=1)
            ordered = jnp.moveaxis(ordered, 2, 0).reshape(history.shape[0], 2, rows_count * half, stop - start)
            arrived[number] = ordered[:, 0], ordered[:, 1]

    def end_past(number, step):
        start, stop = chunks[number]
        return past_call(
            delay,
            tile,
            interaction,
            arrived[number],
            marks[number],
            carried[number],
            incident[:, :, start:stop],
            last,
            (step,),
            layers,
            fanout,
        )

    numbers = range(len(chunks))
    kepts, sents = [None] * len(chunks), [None] * len(chunks)
    for number in numbers:
        kepts[number], sents[number] = folded(*end_past(number, 0))
    gots, laters = [], []
    for number in numbers:
        gots.append(last_hop(sents[number]))
        sents[number], marks[number] = lax.optimization_barrier((sents[number], marks[number]))
        later, gots[number] = lax.optimization_barrier((end_past(number, 1)[0], gots[number]))
        laters.append(later)
    by_layers = [to_layers(load_call(interaction, kepts[number], gots[number], gain, cubic)) for number in numbers]
    every, ends = [], []
    for number in numbers:
        ordered = arrange_call(interaction, [by_layers[number][apart] for apart in range(layers)], fanout)
        if number:
            ordered, ends[-1] = lax.optimization_barrier((ordered, ends[-1]))
        every.append(to_sources(ordered))
        ends.append(
            recent_call(delay, tile, interaction, every[number][0], laters[number], 0, fanout, cols_count)
        )
    for number in numbers:
        for beside in range(1, fanout):
            ends[number] = recent_call(
                delay, tile, interaction, every[number][beside], ends[number][0], beside, fanout, cols_count
            )
        kepts[number], sents[number] = folded(*ends[number])
    gots = [last_hop(sents[number]) for number in numbers]
    lasts = [load_call(interaction, kepts[number], gots[number], gain, cubic) for number in numbers]
    results = [jnp.stack([by_layer[0], last]) for by_layer, last in zip(by_layers, lasts)]
    return jnp.concatenate(results, axis=2)


def solution(mesh):
    placed = (
        P(None, "row", "col"),
        P(None, ("col", "row"), None),
        P(None, ("row", "col"), None),
        P("row"),
        P("row"),
        P("row", "col", None),
        P("row", "col"),
    )
    return jax.shard_map(
        functools.partial(per_device, mesh.shape["row"], mesh.shape["col"]),
        mesh=mesh,
        in_specs=placed,
        out_specs=P(None, ("row", "col"), None),
        check_vma=False,
    )
```
